256 devices in a mesh: row: 32 (over y, z), col: 8 (over x, core).
Axes of the slice: x: 4, y: 4, z: 8, core: 2. Of those that a mesh axis runs over, the one named last changes fastest.
Arguments:
- features: bfloat16 [65536, 128], P(('row', 'col')), may hold values from -6 to 6
- tiles: bfloat16 [32, 8, 128, 128, 128], P('row', 'col'), may hold values from -6 to 6
- block_rows: int32 [32, 8, 128], P('row', 'col'), may hold values from 0 to 15
- block_cols: int32 [32, 8, 128], P('row', 'col'), may hold values from 0 to 63
- labels: int32 [65536], P(('row', 'col')), may hold values from 0 to 171
- train_mask: int32 [65536], P(('row', 'col')), may hold values 0 or 1
- self_first: bfloat16 [128, 256], replicated, may hold values from -0.5 to 0.5
- neigh_first: bfloat16 [128, 256], replicated, may hold values from -0.5 to 0.5
- bias_first: float32 [256], replicated, may hold values from -4 to 4
- self_second: bfloat16 [256, 172], replicated, may hold values from -0.375 to 0.375
- neigh_second: bfloat16 [256, 172], replicated, may hold values from -0.375 to 0.375
- bias_second: float32 [172], replicated, may hold values from -4 to 4
Outputs:
- grad_self_first: float32 [128, 256], replicated
- grad_neigh_first: float32 [128, 256], replicated
- grad_bias_first: float32 [256], replicated
- grad_self_second: float32 [256, 172], replicated
- grad_neigh_second: float32 [256, 172], replicated
- grad_bias_second: float32 [172], replicated
The draws below stay inside these ranges and needn't reach their ends.
All inputs are finite; a program needn't handle non-finite values. No bound on the sum of `train_mask` on one device may be relied on, other than what follows from the above.
Results may differ from the reference program's by a relative error of at most 0.014.
The reference program's roundings to bfloat16 on the way (of `first_agg`, `hidden`, `second_agg`, `logit_grad`, `projected` and `pre_grad`) count: a program that leaves them out, or rounds other values in their place, can miss the bound.
Values may be sent and summed in bfloat16 or wider, within the bound.
No kernel may reach another device: no remote copies, remote signals or barrier semaphores. Data moves between devices by JAX's collectives and lax.ppermute only.
A program may use at most 128 MiB of HBM per device.

```python
import math
import jax
import jax.numpy as jnp
from jax import lax

F_IN = 128
HID = 256
CLASSES = 172
BLOCK = 128
VB = 2
TILES = 128
VERTICES = 65536
N_ROW = 32
N_COL = 8


def set_ends(values, stream_key, smallest, top_value):
    index_at = [jax.random.randint(jax.random.fold_in(stream_key, axis), (), 0, length) for axis, length in enumerate(values.shape)]
    widest = values.shape.index(max(values.shape))
    neighbour = index_at[:widest] + [(index_at[widest] + 1) % values.shape[widest]] + index_at[widest + 1:]
    return values.at[tuple(index_at)].set(smallest).at[tuple(neighbour)].set(top_value)


def block_levels(rng, shape, cuts, low, largest):
    def one(dim, parts):
        heights = jax.random.uniform(jax.random.fold_in(jax.random.fold_in(rng, 6), dim), (parts,), jnp.float32, low / len(cuts), largest / len(cuts))
        return jnp.repeat(jnp.exp(heights), shape[dim] // parts).reshape((-1,) + (1,) * (len(shape) - dim - 1))

    loudness = one(*cuts[0])
    for cut in cuts[1:]:
        loudness = loudness * one(*cut)
    return loudness


def scatter_about(key, extent, width, limit, shards=(), held_as=jnp.bfloat16):
    drawn = width * jax.random.normal(key, extent, jnp.float32)
    if shards:
        drawn = drawn * block_levels(key, extent, shards, -0.22, 0.18)
    return jnp.clip(drawn, -limit, limit).astype(held_as)


def setup_inputs(seed: int = 0) -> dict:
    key_list = jax.random.split(jax.random.key(seed), 13)
    features = scatter_about(key_list[0], (VERTICES, F_IN), 1.0, 6.0, ((0, 256),))
    tiles = scatter_about(key_list[1], (N_ROW, N_COL, TILES, BLOCK, BLOCK), 1.0, 6.0, ((0, 32), (1, 8)))
    block_rows = set_ends(jax.random.randint(key_list[2], (N_ROW, N_COL, TILES), 0, N_COL * VB), jax.random.fold_in(key_list[2], 1), 0, (N_COL * VB) - 1).astype(jnp.int32)
    block_cols = set_ends(jax.random.randint(key_list[3], (N_ROW, N_COL, TILES), 0, N_ROW * VB), jax.random.fold_in(key_list[3], 1), 0, (N_ROW * VB) - 1).astype(jnp.int32)
    labels = set_ends(jax.random.randint(key_list[4], (VERTICES,), 0, CLASSES), jax.random.fold_in(key_list[4], 1), 0, CLASSES - 1).astype(jnp.int32)
    train_mask = set_ends((jax.random.randint(key_list[5], (VERTICES,), 0, 2) < 1).astype(jnp.int32), jax.random.fold_in(key_list[5], 1), 0, 1)
    self_first = scatter_about(key_list[6], (F_IN, HID), F_IN ** -0.5, 0.5)
    neigh_first = scatter_about(key_list[7], (F_IN, HID), F_IN ** -0.5, 0.5)
    bias_first = scatter_about(key_list[8], (HID,), 1.0, 4.0, (), jnp.float32)
    self_second = scatter_about(key_list[9], (HID, CLASSES), HID ** -0.5, 0.375)
    neigh_second = scatter_about(key_list[10], (HID, CLASSES), HID ** -0.5, 0.375)
    bias_second = scatter_about(key_list[11], (CLASSES,), 1.0, 4.0, (), jnp.float32)
    return dict(features=features, tiles=tiles, block_rows=block_rows, block_cols=block_cols, labels=labels, train_mask=train_mask, self_first=self_first, neigh_first=neigh_first, bias_first=bias_first, self_second=self_second, neigh_second=neigh_second, bias_second=bias_second)


def tile_sum(tiles, block_rows, block_cols, source, flipped):
    columns = source.shape[1]
    src_blocks = source.reshape(-1, BLOCK, columns)
    device_count = N_ROW * N_COL
    tile_sets = tiles.reshape(device_count, TILES, BLOCK, BLOCK)
    row_sets = block_rows.reshape(device_count, TILES)
    col_sets = block_cols.reshape(device_count, TILES)
    numbers = jnp.arange(device_count, dtype=jnp.int32)

    def device_step(totals, inputs):
        tile_set, rows_here, cols_here, number = inputs
        row_idx = number // N_COL
        col_idx = number % N_COL
        dest = (row_idx * N_COL * VB + rows_here).astype(jnp.int32)
        anchor = ((cols_here // VB * N_COL + col_idx) * VB + cols_here % VB).astype(jnp.int32)
        tile_float = tile_set.astype(jnp.float32)
        if flipped:
            picked = src_blocks[dest].astype(jnp.float32)
            result = jnp.einsum('tji,tjf->tif', tile_float, picked)
            return (totals.at[anchor].add(result), None)
        picked = src_blocks[anchor].astype(jnp.float32)
        result = jnp.einsum('tij,tjf->tif', tile_float, picked)
        return (totals.at[dest].add(result), None)
    starting = jnp.zeros((src_blocks.shape[0], BLOCK, columns), jnp.float32)
    totals, _ = lax.scan(device_step, starting, (tile_sets, row_sets, col_sets, numbers))
    return totals.reshape(-1, columns)

def reference(features, tiles, block_rows, block_cols, labels, train_mask, self_first, neigh_first, bias_first, self_second, neigh_second, bias_second):
    loss_scale = 1.0 / math.sqrt(VERTICES)
    squares = lax.optimization_barrier(jnp.sum(jnp.square(tiles.astype(jnp.float32)), axis=-1))
    row_base = (jnp.arange(N_ROW, dtype=jnp.int32) * N_COL * VB)[:, None, None]
    dest = (row_base + block_rows).astype(jnp.int32).reshape(-1)
    degree = jnp.zeros((VERTICES // BLOCK, BLOCK), jnp.float32).at[dest].add(squares.reshape(-1, BLOCK)).reshape(-1)
    inverse = lax.rsqrt(1.0 + degree)[:, None]
    first_agg = (inverse * tile_sum(tiles, block_rows, block_cols, features, False)).astype(jnp.bfloat16)
    pre_first = jnp.dot(features, self_first, preferred_element_type=jnp.float32) + jnp.dot(first_agg, neigh_first, preferred_element_type=jnp.float32) + bias_first
    hidden = jax.nn.relu(pre_first).astype(jnp.bfloat16)
    second_agg = (inverse * tile_sum(tiles, block_rows, block_cols, hidden, False)).astype(jnp.bfloat16)
    logits = jnp.dot(hidden, self_second, preferred_element_type=jnp.float32) + jnp.dot(second_agg, neigh_second, preferred_element_type=jnp.float32) + bias_second
    probabilities = jax.nn.softmax(logits, axis=-1)
    onehot = (labels[:, None] == jnp.arange(CLASSES, dtype=jnp.int32)[None, :]).astype(jnp.float32)
    logit_grad = ((probabilities - onehot) * (train_mask.astype(jnp.float32) * loss_scale)[:, None]).astype(jnp.bfloat16)
    projected = (inverse * jnp.dot(logit_grad, neigh_second.T, preferred_element_type=jnp.float32)).astype(jnp.bfloat16)
    backflow = tile_sum(tiles, block_rows, block_cols, projected, True)
    hidden_grad = jnp.dot(logit_grad, self_second.T, preferred_element_type=jnp.float32) + backflow
    pre_grad = jnp.where(pre_first > 0, hidden_grad, 0.0).astype(jnp.bfloat16)
    grad_self_first = jnp.einsum('vi,vj->ij', features, pre_grad, preferred_element_type=jnp.float32)
    grad_neigh_first = jnp.einsum('vi,vj->ij', first_agg, pre_grad, preferred_element_type=jnp.float32)
    grad_bias_first = lax.optimization_barrier(jnp.sum(pre_grad.astype(jnp.float32), axis=0))
    grad_self_second = jnp.einsum('vi,vj->ij', hidden, logit_grad, preferred_element_type=jnp.float32)
    grad_neigh_second = jnp.einsum('vi,vj->ij', second_agg, logit_grad, preferred_element_type=jnp.float32)
    grad_bias_second = lax.optimization_barrier(jnp.sum(logit_grad.astype(jnp.float32), axis=0))
    return (grad_self_first, grad_neigh_first, grad_bias_first, grad_self_second, grad_neigh_second, grad_bias_second)
```

```python
import functools
import math

import jax
import jax.numpy as jnp
from jax import lax
from jax.experimental import pallas as pl
from jax.experimental.pallas import tpu as pltpu
from jax.sharding import PartitionSpec as P

EDGE = 128
PAD = 176
NY, NZ = 4, 8
F32, BF16 = jnp.float32, jnp.bfloat16
VMEM = pl.BlockSpec(memory_space=pltpu.VMEM)
SMEM = pl.BlockSpec(memory_space=pltpu.SMEM)
ANY = pl.BlockSpec(memory_space=pl.ANY)
NT = (((1,), (1,)), ((), ()))


def dot(a, b):
    return jnp.dot(a, b, preferred_element_type=F32)


def dot_nt(a, b):
    return lax.dot_general(a, b, NT, preferred_element_type=F32)


def call(body, out, n_smem, n_in, scratch=(), any_from=None, flops=0, bytes_accessed=0):
    specs = [SMEM] * n_smem + [VMEM] * (n_in - n_smem)
    if any_from is not None:
        specs[any_from:] = [ANY] * (n_in - any_from)
    return pl.pallas_call(
        body,
        out_shape=out,
        in_specs=specs,
        out_specs=jax.tree.map(lambda _: VMEM, out),
        scratch_shapes=list(scratch),
        compiler_params=pltpu.CompilerParams(vmem_limit_bytes=48 * 1024 * 1024),
        cost_estimate=pl.CostEstimate(
            flops=flops, bytes_accessed=bytes_accessed, transcendentals=0
        ),
    )


def step(x, groups, shift):
    pairs = [(g[i], g[(i + shift) % len(g)]) for g in groups for i in range(len(g))]
    return lax.ppermute(x, "row", pairs)


def gather_rows(x):
    along_z = [[NZ * y + z for z in range(NZ)] for y in range(NY)]
    along_y = [[NZ * y + z for y in range(NY)] for z in range(NZ)]
    x = jnp.concatenate(
        [x, step(x, along_y, 1), step(x, along_y, -1), step(x, along_y, 2)], axis=0
    )
    up = down = x
    parts = [x]
    for _ in range(NZ // 2 - 1):
        up, down = step(up, along_z, 1), step(down, along_z, -1)
        parts += [up, down]
    half = x.shape[0] // 2
    parts += [step(up[:half], along_z, 1), step(down[half:], along_z, -1)]
    return parts


def place_of(block, row):
    owner = block // 2
    dz = (owner % NZ - row % NZ) % NZ
    dy = (owner // NZ - row // NZ) % NY
    z_place = jnp.where(dz <= 3, 2 * dz, jnp.where(dz == 4, 7, 15 - 2 * dz))
    y_place = jnp.where(dy == 0, 0, jnp.where(dy == 3, 1, dy + 1))
    return (z_place * NY + y_place) * 2 + block % 2


def block_at(place, row):
    z_place, y_place = place // (2 * NY), place // 2 % NY
    dz = jnp.where(z_place == 7, 4, jnp.where(z_place % 2 == 0, z_place // 2, 8 - (z_place + 1) // 2))
    dy = jnp.where(y_place == 0, 0, jnp.where(y_place == 1, 3, y_place - 1))
    z = (row % NZ + dz) % NZ
    y = (row // NZ + dy) % NY
    return (y * NZ + z) * 2 + place % 2


def start_parts(parts, held, sem):
    copies, at = [], 0
    for p in parts:
        n = p.shape[0]
        copies.append(pltpu.make_async_copy(p, held.at[pl.ds(at, n)], sem.at[len(copies)]))
        copies[-1].start()
        at += n
    return copies


def degree_kernel(rows, tiles, out):
    out[...] = jnp.zeros_like(out)
    ones = jnp.ones((8, EDGE), BF16)

    def body(t, carry):
        x = tiles[t].astype(F32)
        x = x * x
        hi = x.astype(BF16)
        lo = (x - hi.astype(F32)).astype(BF16)
        out[rows[t]] += dot_nt(ones, hi) + dot_nt(ones, lo)
        return carry

    lax.fori_loop(0, tiles.shape[0], body, 0, unroll=4)


def first_kernel(n_parts, offs, cols, tiles, deg, *refs):
    parts, out, held, sem = refs[:n_parts], refs[n_parts], refs[n_parts + 1], refs[n_parts + 2]
    copies = start_parts(parts, held, sem)
    out[...] = jnp.zeros_like(out)
    for g in range(8):
        for b in range(2):
            out[pl.ds(g * 264 + 256 + b, 1), :] = deg[2 * g + b][:1]
    for c in copies:
        c.wait()
    unroll = 4

    def body(i, carry):
        got = [dot(tiles[i * unroll + u], held[cols[i * unroll + u]]) for u in range(unroll)]
        for u in range(unroll):
            at = pl.ds(pl.multiple_of(offs[i * unroll + u], 8), EDGE)
            out[at, :] += got[u]
        return carry

    lax.fori_loop(0, tiles.shape[0] // unroll, body, 0)


def hidden_kernel(sums, features, self_first, neigh_first, bias, agg, hid, inv):
    total = sums[0]
    for g in range(1, 8):
        total = total + sums[g]
    for b in range(2):
        x = 1.0 + total[256 + b : 257 + b]
        r = lax.rsqrt(x)
        r = r * (1.5 - 0.5 * x * r * r)
        inv[pl.ds(b, 1), :] = r
        column = jnp.broadcast_to(r, (EDGE, EDGE)).T
        agg[b] = (column * total[b * EDGE : (b + 1) * EDGE]).astype(BF16)
        pre = (
            dot_nt(self_first[...], features[b])
            + dot_nt(neigh_first[...], agg[b])
            + bias[...]
        )
        hid[b] = jnp.maximum(pre, 0.0).astype(BF16)


def second_kernel(n_parts, rows, cols, tiles, neigh, *refs):
    parts, agg, logit, held, acc, sem = refs[:n_parts], *refs[n_parts:]
    copies = start_parts(parts, held, sem)
    acc[...] = jnp.zeros_like(acc)
    for c in copies:
        c.wait()
    unroll = 2

    def body(i, carry):
        got = [dot_nt(held[cols[i * unroll + u]], tiles[i * unroll + u]) for u in range(unroll)]
        for u in range(unroll):
            acc[rows[i * unroll + u]] += got[u]
        return carry

    lax.fori_loop(0, tiles.shape[0] // unroll, body, 0)

    def finish(d, carry):
        agg[d] = acc[d].astype(BF16)
        logit[d] = dot(neigh[...], agg[d]).astype(BF16)
        return carry

    lax.fori_loop(0, 16, finish, 0, unroll=2)


def loss_kernel(classes, scale, parts, hid, self_t, bias, labels, mask, inv, lg, w, grad, grad_bias):
    rows = lax.broadcasted_iota(jnp.int32, (PAD, EDGE), 0)
    ones = jnp.ones((8, EDGE), BF16)
    for b in range(2):
        total = parts[0, b].astype(F32)
        for g in range(1, 8):
            total = total + parts[g, b].astype(F32)
        factor = inv[b : b + 1]
        logits = dot(self_t[...], hid[b]) + factor * total + bias[...]
        logits = jnp.where(rows < classes, logits, -1e30)
        e = jnp.exp(logits - jnp.max(logits, axis=0, keepdims=True))
        p = e / jnp.sum(e, axis=0, keepdims=True)
        p = p - jnp.where(rows == labels[b : b + 1], 1.0, 0.0)
        got = (p * (mask[b : b + 1].astype(F32) * scale)).astype(BF16)
        lg[b] = got
        w[b] = (got.astype(F32) * factor).astype(BF16)
        if b == 0:
            grad[...] = dot_nt(got, hid[b])
            grad_bias[...] = dot_nt(ones, got)
        else:
            grad[...] += dot_nt(got, hid[b])
            grad_bias[...] += dot_nt(ones, got)


def last_kernel(
    n_parts, rows, cols, order, tiles, w, agg_second, lg, self_second, neigh_second,
    grad_self, grad_bias, feat, agg_first, *refs
):
    parts, out, held, acc, proj, g_neigh, g_first, g_bias, sem = refs[:n_parts], *refs[n_parts:]
    copies = start_parts(parts, held, sem)

    def project(d, carry):
        proj[d] = dot(neigh_second[...], w[d]).astype(BF16)
        got = dot_nt(w[d], agg_second[d])
        g_neigh[...] = jnp.where(d == 0, 0.0, g_neigh[...]) + got
        return carry

    g_neigh[...] = jnp.zeros_like(g_neigh)
    lax.fori_loop(0, 16, project, 0)
    acc[...] = jnp.zeros_like(acc)
    for b in range(2):
        acc[b] = dot(self_second[...], lg[b])
    unroll = 2

    def body(i, carry):
        got = [dot(proj[rows[i * unroll + u]], tiles[i * unroll + u]) for u in range(unroll)]
        for u in range(unroll):
            acc[cols[i * unroll + u]] += got[u]
        return carry

    lax.fori_loop(0, tiles.shape[0] // unroll, body, 0)
    for c in copies:
        c.wait()
    ones = jnp.ones((8, EDGE), BF16)
    g_first[...] = jnp.zeros_like(g_first)
    g_bias[...] = jnp.zeros_like(g_bias)

    def contract(s, carry):
        p = jnp.where(held[s].astype(F32) > 0.0, acc[s], 0.0).astype(BF16)
        g_first[0] += dot(p, feat[s])
        g_first[1] += dot(p, agg_first[order[s]])
        g_bias[...] += dot_nt(ones, p)
        return carry

    lax.fori_loop(0, 64, contract, 0)
    out[pl.ds(0, 256), :] = g_first[0].astype(BF16)
    out[pl.ds(256, 256), :] = g_first[1].astype(BF16)
    for i in range(2):
        lanes = slice(i * EDGE, (i + 1) * EDGE)
        out[pl.ds(512 + i * PAD, PAD), :] = grad_self[:, lanes].astype(BF16)
        out[pl.ds(512 + (2 + i) * PAD, PAD), :] = g_neigh[:, lanes].astype(BF16)
    pick = lax.broadcasted_iota(jnp.int32, (16, EDGE), 0)
    zeros = jnp.zeros((1, 256 - PAD), F32)
    second = jnp.concatenate([grad_bias[:1], zeros], axis=1)
    last = jnp.where(
        pick == 0,
        g_bias[:1, :EDGE],
        jnp.where(
            pick == 1,
            g_bias[:1, EDGE:],
            jnp.where(pick == 2, second[:, :EDGE], jnp.where(pick == 3, second[:, EDGE:], 0.0)),
        ),
    )
    out[pl.ds(512 + 4 * PAD, 16), :] = last.astype(BF16)
    out[pl.ds(512 + 4 * PAD + 16, 1280 - 528 - 4 * PAD), :] = jnp.zeros(
        (1280 - 528 - 4 * PAD, EDGE), BF16
    )


def on_device(
    features,
    tiles,
    block_rows,
    block_cols,
    labels,
    train_mask,
    self_first,
    neigh_first,
    bias_first,
    self_second,
    neigh_second,
    bias_second,
):
    classes = self_second.shape[1]
    hid_size = self_first.shape[1]
    scale = 1.0 / math.sqrt(65536)
    row = lax.axis_index("row")
    tiles = tiles.reshape(-1, EDGE, EDGE)
    rows = block_rows.reshape(-1)
    cols = place_of(block_cols.reshape(-1), row)
    offs = rows // 2 * 264 + rows % 2 * EDGE
    order = block_at(jnp.arange(64, dtype=jnp.int32), row)
    shape = jax.ShapeDtypeStruct
    feat = features.reshape(2, EDGE, EDGE)

    feat_parts = gather_rows(feat)
    n_parts = len(feat_parts)
    sems = pltpu.SemaphoreType.DMA((n_parts,))
    deg = call(degree_kernel, shape((16, 8, EDGE), F32), 1, 2, flops=2**28, bytes_accessed=2**22)(
        rows, tiles
    )
    first = call(
        functools.partial(first_kernel, n_parts),
        shape((8 * 264, EDGE), F32),
        2,
        4 + n_parts,
        [pltpu.VMEM((64, EDGE, EDGE), BF16), sems],
        any_from=4,
        flops=2**29,
        bytes_accessed=2**23,
    )(offs, cols, tiles, deg, *feat_parts)
    sums = lax.all_to_all(first.reshape(8, 264, EDGE), "col", 0, 0, tiled=True)
    agg, hid, inv = call(
        hidden_kernel,
        (
            shape((2, EDGE, EDGE), BF16),
            shape((2, hid_size, EDGE), BF16),
            shape((2, EDGE), F32),
        ),
        0,
        5,
    )(
        sums,
        feat,
        self_first.T,
        neigh_first.T,
        jnp.broadcast_to(bias_first[:, None], (hid_size, EDGE)),
    )
    hid_parts = gather_rows(hid)
    agg_first = lax.all_gather(agg, "row", axis=0, tiled=True)

    wide = ((0, 0), (0, PAD - classes))
    self_wide = jnp.pad(self_second, wide)
    neigh_wide = jnp.pad(neigh_second, wide)
    bias_wide = jnp.broadcast_to(jnp.pad(bias_second, (0, PAD - classes))[:, None], (PAD, EDGE))
    agg_second, partial = call(
        functools.partial(second_kernel, n_parts),
        (shape((16, hid_size, EDGE), BF16), shape((16, PAD, EDGE), BF16)),
        2,
        4 + n_parts,
        [pltpu.VMEM((64, hid_size, EDGE), BF16), pltpu.VMEM((16, hid_size, EDGE), F32), sems],
        any_from=4,
        flops=2**30,
        bytes_accessed=2**23,
    )(rows, cols, tiles, neigh_wide.T, *hid_parts)
    partial = lax.all_to_all(partial.reshape(8, 2, PAD, EDGE), "col", 0, 0, tiled=True)
    lg, w, grad_self, grad_bias = call(
        functools.partial(loss_kernel, classes, scale),
        (
            shape((2, PAD, EDGE), BF16),
            shape((2, PAD, EDGE), BF16),
            shape((PAD, hid_size), F32),
            shape((8, PAD), F32),
        ),
        0,
        7,
    )(
        partial,
        hid,
        self_wide.T,
        bias_wide,
        labels.reshape(2, EDGE),
        train_mask.reshape(2, EDGE),
        inv,
    )
    w_all = lax.all_gather(w, "col", axis=0, tiled=True)
    grads = call(
        functools.partial(last_kernel, n_parts),
        shape((1280, EDGE), BF16),
        3,
        13 + n_parts,
        [
            pltpu.VMEM((64, hid_size, EDGE), BF16),
            pltpu.VMEM((64, hid_size, EDGE), F32),
            pltpu.VMEM((16, hid_size, EDGE), BF16),
            pltpu.VMEM((PAD, hid_size), F32),
            pltpu.VMEM((2, hid_size, EDGE), F32),
            pltpu.VMEM((8, hid_size), F32),
            sems,
        ],
        any_from=13,
        flops=2**31,
        bytes_accessed=2**24,
    )(
        rows, cols, order, tiles, w_all, agg_second, lg, self_wide, neigh_wide,
        grad_self, grad_bias, jnp.concatenate(feat_parts, axis=0), agg_first, *hid_parts
    )
    every = ("row", "col")
    mine = lax.all_to_all(grads.reshape(256, 5, EDGE), every, 0, 0, tiled=True)
    mine = jnp.sum(mine.astype(F32), axis=0).astype(BF16)
    full = lax.all_to_all(jnp.broadcast_to(mine[None], (256, 5, EDGE)), every, 0, 0, tiled=True)
    full = full.reshape(1280, EDGE).astype(F32)
    half = lambda at, n: jnp.concatenate([full[at : at + n], full[at + PAD : at + PAD + n]], axis=1)
    end = 512 + 4 * PAD
    return (
        full[:256].T,
        full[256:512].T,
        full[end : end + 2].reshape(hid_size),
        half(512, classes).T,
        half(512 + 2 * PAD, classes).T,
        full[end + 2 : end + 4].reshape(256)[:classes],
    )


def solution(mesh):
    in_specs = (
        P(("row", "col"), None),
        P("row", "col", None, None, None),
        P("row", "col", None),
        P("row", "col", None),
        P(("row", "col")),
        P(("row", "col")),
        P(),
        P(),
        P(),
        P(),
        P(),
        P(),
    )
    out_specs = (P(), P(), P(), P(), P(), P())
    return jax.shard_map(
        on_device, mesh=mesh, in_specs=in_specs, out_specs=out_specs, check_vma=False
    )
```

```python
import functools
import math

import jax
import jax.numpy as jnp
from jax import lax
from jax.experimental import pallas as pl
from jax.experimental.pallas import tpu as pltpu
from jax.sharding import PartitionSpec as P

EDGE = 128
GROUP = 32
PAD = 176
NY, NZ = 4, 8
F32, BF16 = jnp.float32, jnp.bfloat16
VMEM = pl.BlockSpec(memory_space=pltpu.VMEM)
SMEM = pl.BlockSpec(memory_space=pltpu.SMEM)
ANY = pl.BlockSpec(memory_space=pl.ANY)
HBM = pl.BlockSpec(memory_space=pltpu.HBM)
NT = (((1,), (1,)), ((), ()))


def dot(a, b):
    return jnp.dot(a, b, preferred_element_type=F32)


def dot_nt(a, b):
    return lax.dot_general(a, b, NT, preferred_element_type=F32)


def call(body, out, specs, scratch=(), mib=4, flops=0, bytes_accessed=0):
    return pl.pallas_call(
        body,
        out_shape=out,
        in_specs=specs,
        out_specs=jax.tree.map(lambda _: VMEM, out),
        scratch_shapes=list(scratch),
        compiler_params=pltpu.CompilerParams(vmem_limit_bytes=mib * 1024 * 1024),
        cost_estimate=pl.CostEstimate(
            flops=flops, bytes_accessed=bytes_accessed, transcendentals=0
        ),
    )


def step(x, groups, shift):
    pairs = [(g[i], g[(i + shift) % len(g)]) for g in groups for i in range(len(g))]
    return lax.ppermute(x, "row", pairs)


ALONG_Z = [[NZ * y + z for z in range(NZ)] for y in range(NY)]
ALONG_Y = [[NZ * y + z for y in range(NY)] for z in range(NZ)]


def ring(x, groups):
    count = len(groups[0])
    up = down = x
    parts = [x]
    for _ in range(count // 2 - 1):
        up, down = step(up, groups, 1), step(down, groups, -1)
        parts += [up, down]
    half = x.shape[0] // 2
    return parts + [step(up[:half], groups, 1), step(down[half:], groups, -1)]


def along_y(x):
    return [x, step(x, ALONG_Y, 1), step(x, ALONG_Y, -1), step(x, ALONG_Y, 2)]


def place_of(block, row):
    owner = block // 2
    dz = (owner % NZ + NZ - row % NZ) % NZ
    dy = (owner // NZ + NY - row // NZ) % NY
    z_place = jnp.where(dz <= 3, 2 * dz, jnp.where(dz == 4, 7, 15 - 2 * dz))
    y_place = jnp.where(dy == 0, 0, jnp.where(dy == 3, 1, dy + 1))
    return z_place * NY + y_place


def owner_at(place, row):
    z_place, y_place = place // NY, place % NY
    dz = jnp.where(z_place == 7, 4, jnp.where(z_place % 2 == 0, z_place // 2, 8 - (z_place + 1) // 2))
    dy = jnp.where(y_place == 0, 0, jnp.where(y_place == 1, 3, y_place - 1))
    return (row // NZ + dy) % NY * NZ + (row + dz) % NZ


def slot_of(block, col):
    owner = block // 2
    dx = (owner // 2 + 4 - col // 2) % 4
    dc = (owner + col) % 2
    return (dc * 4 + dx) * 2 + block % 2


def to_sibling(x):
    return lax.ppermute(x, "col", [(i, i ^ 1) for i in range(8)])


def along_x(x, shift):
    return lax.ppermute(x, "col", [(i, (i + 2 * shift) % 8) for i in range(8)])


def start_parts(parts, held, sems):
    copies, at = [], 0
    for i, p in enumerate(parts):
        n = p.shape[0]
        copies.append(pltpu.make_async_copy(p, held.at[pl.ds(at, n)], sems.at[i]))
        copies[-1].start()
        at += n
    return copies


def start_tiles(tiles, held, sems):
    copies = []
    for i in range(held.shape[0] // GROUP):
        at = pl.ds(i * GROUP, GROUP)
        copies.append(pltpu.make_async_copy(tiles.at[at], held.at[at], sems.at[i]))
        copies[-1].start()
    return copies


def start_all(pairs, sems):
    copies = [pltpu.make_async_copy(a, b, sems.at[i]) for i, (a, b) in enumerate(pairs)]
    for c in copies:
        c.start()
    return copies


def accumulate(tiles, held, sems, product, add):
    def body(i, carry):
        at = pl.ds(i * GROUP, GROUP)
        pltpu.make_async_copy(tiles.at[at], held.at[at], sems.at[i]).wait()
        got = [product(i * GROUP + u) for u in range(GROUP)]
        for u in range(GROUP):
            add(i * GROUP + u, got[u])
        return carry

    lax.fori_loop(0, held.shape[0] // GROUP, body, 0)


def degree_kernel(first, slots, tiles, out, held, sem):
    tiles = tiles.at[pl.ds(first, GROUP)]
    start_tiles(tiles, held, sem)
    out[...] = jnp.zeros_like(out)
    ones = jnp.ones((8, EDGE), BF16)

    def product(t):
        x = held[t].astype(F32)
        x = x * x
        hi = x.astype(BF16)
        lo = (x - hi.astype(F32)).astype(BF16)
        return dot_nt(ones, hi) + dot_nt(ones, lo)

    def add(t, got):
        out[slots[first + t]] += got

    accumulate(tiles, held, sem, product, add)


def first_kernel(n_parts, offs, cols, tiles_hbm, d0, d1, d2, d3, *refs):
    parts, keep, send, tiles, held, acc, tile_sem, sem = refs[:n_parts], *refs[n_parts:]
    copies = start_parts(parts, held, sem)
    start_tiles(tiles_hbm, tiles, tile_sem)
    acc[...] = jnp.zeros_like(acc)
    for s in range(16):
        deg = (d0[s][:1] + d1[s][:1]) + (d2[s][:1] + d3[s][:1])
        acc[pl.ds(s // 2 * 264 + 256 + s % 2, 1), :] = deg
    for c in copies:
        c.wait()

    def add(t, got):
        acc[pl.ds(pl.multiple_of(offs[t], 8), EDGE), :] += got

    accumulate(tiles_hbm, tiles, tile_sem, lambda t: dot(tiles[t], held[cols[t]]), add)
    keep[...] = acc[pl.ds(0, 1056), :]
    send[...] = acc[pl.ds(1056, 1056), :]


def join_first_kernel(keep, got, *out):
    for x in range(4):
        at = pl.ds(x * 264, 264)
        out[x][...] = keep[at, :] + got[at, :]


def flip(x):
    return x.astype(F32).T


def hidden_kernel(s0, s1, s2, s3, features, self_first, neigh_first, bias, agg, hid, inv):
    total = (s0[...] + s1[...]) + (s2[...] + s3[...])
    self_t, neigh_t = flip(self_first[...]).astype(BF16), flip(neigh_first[...]).astype(BF16)
    bias_t = jnp.broadcast_to(bias[...], (EDGE, bias.shape[1])).T
    for b in range(2):
        x = 1.0 + total[256 + b : 257 + b]
        r = lax.rsqrt(x)
        r = r * (1.5 - 0.5 * x * r * r)
        inv[pl.ds(b, 1), :] = r
        column = jnp.broadcast_to(r, (EDGE, EDGE)).T
        agg[b] = (column * total[b * EDGE : (b + 1) * EDGE]).astype(BF16)
        pre = dot_nt(self_t, features[b]) + dot_nt(neigh_t, agg[b]) + bias_t
        hid[b] = jnp.maximum(pre, 0.0).astype(BF16)


def second_kernel(n_parts, slots, cols, tiles_hbm, neigh_hbm, *refs):
    parts, agg, keep, send = refs[:n_parts], *refs[n_parts : n_parts + 3]
    tiles, neigh, held, acc, tile_sem, sem, neigh_sem = refs[n_parts + 3 :]
    copies = start_parts(parts, held, sem)
    start_tiles(tiles_hbm, tiles, tile_sem)
    neigh_copy = pltpu.make_async_copy(neigh_hbm, neigh, neigh_sem)
    neigh_copy.start()
    acc[...] = jnp.zeros_like(acc)
    for c in copies:
        c.wait()

    def add(t, got):
        acc[slots[t]] += got

    accumulate(tiles_hbm, tiles, tile_sem, lambda t: dot_nt(held[cols[t]], tiles[t]), add)
    neigh_copy.wait()
    for s in range(16):
        agg[s] = acc[s].astype(BF16)
        got = dot(neigh[pl.ds(0, PAD), :], agg[s]).astype(BF16)
        if s < 8:
            keep[s] = got
        else:
            send[s - 8] = got


def join_second_kernel(keep, got, *out):
    for s in range(8):
        out[s // 2][s % 2] = (keep[s].astype(F32) + got[s].astype(F32)).astype(BF16)


def loss_kernel(
    classes, scale, s0, s1, s2, s3, hid, self_t, bias, labels, mask, inv, lg, w, grad, grad_bias
):
    rows = lax.broadcasted_iota(jnp.int32, (PAD, EDGE), 0)
    ones = jnp.ones((8, EDGE), BF16)
    for b in range(2):
        total = (s0[b].astype(F32) + s1[b].astype(F32)) + (s2[b].astype(F32) + s3[b].astype(F32))
        factor = inv[b : b + 1]
        logits = dot(self_t[pl.ds(0, PAD), :], hid[b]) + factor * total + bias[...]
        logits = jnp.where(rows < classes, logits, -1e30)
        e = jnp.exp(logits - jnp.max(logits, axis=0, keepdims=True))
        p = e / jnp.sum(e, axis=0, keepdims=True)
        p = p - jnp.where(rows == labels[b : b + 1], 1.0, 0.0)
        got = (p * (mask[b : b + 1].astype(F32) * scale)).astype(BF16)
        lg[b] = got
        w[b] = (got.astype(F32) * factor).astype(BF16)
        if b == 0:
            grad[...] = dot_nt(got, hid[b])
            grad_bias[...] = dot_nt(ones, got)
        else:
            grad[...] += dot_nt(got, hid[b])
            grad_bias[...] += dot_nt(ones, got)


X_ORDER = (0, 3, 1, 2)


def last_kernel(
    n_feat, n_hid, slots, cols, order, w0, w1, w2, w3, tiles_hbm, agg_second_hbm, lg_hbm, self_hbm,
    neigh_hbm, grad_self_hbm, grad_bias, agg_first_hbm, *refs
):
    feat_parts, hid_parts = refs[:n_feat], refs[n_feat : n_feat + n_hid]
    (
        out, tiles, agg_second, lg, self_t, neigh_t, grad_self, agg_first, feat, held, acc, proj,
        tile_sem, feat_sem, hid_sem, sems,
    ) = refs[n_feat + n_hid :]
    pairs = (
        (neigh_hbm, neigh_t),
        (agg_second_hbm, agg_second),
        (lg_hbm, lg),
        (self_hbm, self_t),
        (grad_self_hbm, grad_self),
        (agg_first_hbm, agg_first),
    )
    small = start_all(pairs, sems)
    start_tiles(tiles_hbm, tiles, tile_sem)
    copies = start_parts(hid_parts, held, hid_sem) + start_parts(feat_parts, feat, feat_sem)
    acc[...] = jnp.zeros_like(acc)
    for c in small[:5]:
        c.wait()
    lacking = jnp.zeros((256 - PAD, EDGE), BF16)
    self_second = flip(self_t[...]).astype(BF16)
    neigh_second = flip(neigh_t[...]).astype(BF16)
    for b in range(2):
        acc[32 * b] = dot(self_second, jnp.concatenate([lg[b], lacking], axis=0))
    g_neigh = jnp.zeros((PAD, 256), F32)
    for dx, part in zip(X_ORDER, (w0, w1, w2, w3)):
        at = [(i // 2 * 4 + dx) * 2 + i % 2 for i in range(4)]
        w = jnp.concatenate([part[i] for i in range(4)], axis=1)
        tall = jnp.concatenate([w, jnp.concatenate([lacking] * 4, axis=1)], axis=0)
        got = dot(neigh_second, tall).astype(BF16)
        for i in range(4):
            proj[at[i]] = got[:, i * EDGE : (i + 1) * EDGE]
        g_neigh += dot_nt(w, jnp.concatenate([agg_second[s] for s in at], axis=1))
    for i in range(2):
        lanes = slice(i * EDGE, (i + 1) * EDGE)
        out[pl.ds(512 + i * PAD, PAD), :] = grad_self[:, lanes].astype(BF16)
        out[pl.ds(512 + (2 + i) * PAD, PAD), :] = g_neigh[:, lanes].astype(BF16)

    def add(t, got):
        acc[cols[t]] += got

    accumulate(tiles_hbm, tiles, tile_sem, lambda t: dot(proj[slots[t]], tiles[t]), add)
    for c in copies + small[5:]:
        c.wait()
    wide = 8
    ones = jnp.ones((8, wide * EDGE), BF16)

    def contract(i, carry):
        g_first, g_bias = carry
        p, f = [], []
        for q in range(wide):
            s = i * wide + q
            p.append(jnp.where(held[s] > 0, acc[s].astype(BF16), jnp.zeros((), BF16)))
            f.append(jnp.concatenate([feat[s % 32 * 2 + s // 32], agg_first[order[s]]], axis=1))
        p = jnp.concatenate(p, axis=1)
        return g_first + dot(p, jnp.concatenate(f, axis=0)), g_bias + dot_nt(ones, p)

    zeros = (jnp.zeros((256, 256), F32), jnp.zeros((8, 256), F32))
    g_first, g_bias = lax.fori_loop(0, 64 // wide, contract, zeros)
    out[pl.ds(0, 256), :] = g_first[:, :EDGE].astype(BF16)
    out[pl.ds(256, 256), :] = g_first[:, EDGE:].astype(BF16)
    pick = lax.broadcasted_iota(jnp.int32, (16, EDGE), 0)
    second = jnp.concatenate([grad_bias[:1], jnp.zeros((1, 256 - PAD), F32)], axis=1)
    rows = (g_bias[:1, :EDGE], g_bias[:1, EDGE:], second[:, :EDGE], second[:, EDGE:])
    last = jnp.zeros((16, EDGE), F32)
    for i, row in enumerate(rows):
        last = jnp.where(pick == i, row, last)
    end = 512 + 4 * PAD
    out[pl.ds(end, 16), :] = last.astype(BF16)
    out[pl.ds(end + 16, 1280 - 16 - end), :] = jnp.zeros((1280 - 16 - end, EDGE), BF16)


def add_pieces_kernel(x, out):
    total = x[0].astype(F32)
    for i in range(1, x.shape[0]):
        total = total + x[i].astype(F32)
    out[...] = total.astype(BF16)


def spread_kernel(a, b, out):
    total = (a[...].astype(F32) + b[...].astype(F32)).astype(BF16)
    for i in range(out.shape[0]):
        out[i] = total


def unpack_kernel(classes, x, self_first, neigh_first, bias_first, self_t, neigh_t, bias_second):
    self_first[...] = flip(x[pl.ds(0, 256), :])
    neigh_first[...] = flip(x[pl.ds(256, 256), :])
    for at, out in ((512, self_t), (512 + 2 * PAD, neigh_t)):
        for i in range(2):
            got = x[pl.ds(at + i * PAD, PAD), :].astype(F32)
            out[:, i * EDGE : (i + 1) * EDGE] = got[:classes]
    last = x[pl.ds(512 + 4 * PAD, 16), :].astype(F32)
    bias_first[...] = jnp.concatenate([last[0:1], last[1:2]], axis=1)
    bias_second[...] = jnp.concatenate([last[2:3], last[3:4]], axis=1)


def sum_everywhere(x):
    every = ("row", "col")
    number = lambda y, z, x, c: ((y * NZ + z) * 4 + x) * 2 + c
    groups = [
        [number(y, z, x, c) for y in range(NY) for x in range(4)] for z in range(NZ) for c in range(2)
    ]
    x = x.reshape(16, -1, EDGE)
    piece = jax.ShapeDtypeStruct(x.shape[1:], BF16)
    x = lax.all_to_all(x, every, 0, 0, tiled=True, axis_index_groups=groups)
    x = call(add_pieces_kernel, piece, [VMEM])(x)
    x = jnp.broadcast_to(x[None], (NZ,) + x.shape)
    x = lax.all_to_all(x, "row", 0, 0, tiled=True, axis_index_groups=ALONG_Z)
    x = call(add_pieces_kernel, piece, [VMEM])(x)
    x = call(spread_kernel, jax.ShapeDtypeStruct((16, 80, EDGE), BF16), [VMEM] * 2)(x, to_sibling(x))
    x = lax.all_to_all(x, every, 0, 0, tiled=True, axis_index_groups=groups)
    return x.reshape(-1, EDGE)


def on_device(
    features,
    tiles,
    block_rows,
    block_cols,
    labels,
    train_mask,
    self_first,
    neigh_first,
    bias_first,
    self_second,
    neigh_second,
    bias_second,
):
    classes = self_second.shape[1]
    hid_size = self_first.shape[1]
    scale = 1.0 / math.sqrt(65536)
    row, col = lax.axis_index("row"), lax.axis_index("col")
    tiles = tiles.reshape(-1, EDGE, EDGE)
    slots = slot_of(block_rows.reshape(-1), col)
    sources = block_cols.reshape(-1)
    place = place_of(sources, row)
    feat_cols, cols = place * 2 + sources % 2, sources % 2 * 32 + place
    offs = slots // 2 * 264 + slots % 2 * EDGE
    spot = jnp.arange(64, dtype=jnp.int32)
    order = owner_at(spot % 32, row) * 2 + spot // 32
    shape = jax.ShapeDtypeStruct
    dma = pltpu.SemaphoreType.DMA
    feat = features.reshape(2, EDGE, EDGE)
    tile_buffer = pltpu.VMEM(tiles.shape, BF16)
    n_groups = tiles.shape[0] // GROUP

    feat_parts = ring(jnp.concatenate(along_y(feat), axis=0), ALONG_Z)
    n_feat = len(feat_parts)
    degs = [
        call(
            functools.partial(degree_kernel, i * GROUP),
            shape((16, 8, EDGE), F32),
            [SMEM, HBM],
            [pltpu.VMEM((GROUP, EDGE, EDGE), BF16), dma((1,))],
            mib=60,
            flops=2**32,
            bytes_accessed=2**20,
        )(slots, tiles)
        for i in range(n_groups)
    ]
    block = shape((1056, EDGE), F32)
    keep, send = call(
        functools.partial(first_kernel, n_feat),
        (block, block),
        [SMEM, SMEM, HBM] + [VMEM] * 4 + [ANY] * n_feat,
        [
            tile_buffer,
            pltpu.VMEM((64, EDGE, EDGE), BF16),
            pltpu.VMEM((2112, EDGE), F32),
            dma((n_groups,)),
            dma((n_feat,)),
        ],
        mib=60,
        flops=2**29,
        bytes_accessed=2**23,
    )(offs, feat_cols, tiles, *degs, *feat_parts)
    sums = call(join_first_kernel, (shape((264, EDGE), F32),) * 4, [VMEM] * 2)(
        keep, to_sibling(send)
    )
    agg, hid, inv = call(
        hidden_kernel,
        (
            shape((2, EDGE, EDGE), BF16),
            shape((2, hid_size, EDGE), BF16),
            shape((2, EDGE), F32),
        ),
        [VMEM] * 8,
    )(
        sums[0],
        along_x(sums[1], 1),
        along_x(sums[2], 2),
        along_x(sums[3], 3),
        feat,
        self_first,
        neigh_first,
        bias_first.reshape(1, -1),
    )
    hid_y, hid_parts = along_y(hid), []
    for b in range(2):
        hid_parts += ring(jnp.concatenate([h[b : b + 1] for h in hid_y], axis=0), ALONG_Z)
    n_hid = len(hid_parts)
    agg_first = lax.all_gather(agg, "row", axis=0, tiled=True)

    lacking = ((0, 256 - classes), (0, 0))
    self_t = jnp.pad(self_second.T, lacking)
    neigh_t = jnp.pad(neigh_second.T, lacking)
    bias_wide = jnp.broadcast_to(jnp.pad(bias_second, (0, PAD - classes))[:, None], (PAD, EDGE))
    half = shape((8, PAD, EDGE), BF16)
    agg_second, keep, send = call(
        functools.partial(second_kernel, n_hid),
        (shape((16, hid_size, EDGE), BF16), half, half),
        [SMEM, SMEM, HBM, HBM] + [ANY] * n_hid,
        [
            tile_buffer,
            pltpu.VMEM((256, hid_size), BF16),
            pltpu.VMEM((64, hid_size, EDGE), BF16),
            pltpu.VMEM((16, hid_size, EDGE), F32),
            dma((n_groups,)),
            dma((n_hid,)),
            dma(()),
        ],
        mib=60,
        flops=2**30,
        bytes_accessed=2**23,
    )(slots, cols, tiles, neigh_t, *hid_parts)
    sums = call(join_second_kernel, (shape((2, PAD, EDGE), BF16),) * 4, [VMEM] * 2)(
        keep, to_sibling(send)
    )
    lg, w, grad_self, grad_bias = call(
        functools.partial(loss_kernel, classes, scale),
        (
            shape((2, PAD, EDGE), BF16),
            shape((2, PAD, EDGE), BF16),
            shape((PAD, hid_size), F32),
            shape((8, PAD), F32),
        ),
        [VMEM] * 10,
    )(
        sums[0],
        along_x(sums[1], 1),
        along_x(sums[2], 2),
        along_x(sums[3], 3),
        hid,
        self_t,
        bias_wide,
        labels.reshape(2, EDGE),
        train_mask.reshape(2, EDGE),
        inv,
    )
    w = jnp.concatenate([w, to_sibling(w)], axis=0)
    w_parts = [w, along_x(w, 1), along_x(w, 3), along_x(w, 2)]
    grads = call(
        functools.partial(last_kernel, n_feat, n_hid),
        shape((1280, EDGE), BF16),
        [SMEM] * 3 + [VMEM] * 4 + [HBM] * 6 + [VMEM, HBM] + [HBM] * (n_feat + n_hid),
        [
            tile_buffer,
            pltpu.VMEM((16, hid_size, EDGE), BF16),
            pltpu.VMEM((2, PAD, EDGE), BF16),
            pltpu.VMEM((256, hid_size), BF16),
            pltpu.VMEM((256, hid_size), BF16),
            pltpu.VMEM((PAD, hid_size), F32),
            pltpu.VMEM((64, EDGE, EDGE), BF16),
            pltpu.VMEM((64, EDGE, EDGE), BF16),
            pltpu.VMEM((64, hid_size, EDGE), BF16),
            pltpu.VMEM((64, hid_size, EDGE), F32),
            pltpu.VMEM((16, hid_size, EDGE), BF16),
            dma((n_groups,)),
            dma((n_feat,)),
            dma((n_hid,)),
            dma((6,)),
        ],
        mib=60,
        flops=2**31,
        bytes_accessed=2**24,
    )(
        slots, cols, order, *w_parts, tiles, agg_second, lg, self_t, neigh_t, grad_self,
        grad_bias, agg_first, *feat_parts, *hid_parts
    )
    out = call(
        functools.partial(unpack_kernel, classes),
        (
            shape(self_first.shape, F32),
            shape(neigh_first.shape, F32),
            shape((1, hid_size), F32),
            shape((classes, hid_size), F32),
            shape((classes, hid_size), F32),
            shape((1, 256), F32),
        ),
        [VMEM],
    )(sum_everywhere(grads))
    return (
        out[0],
        out[1],
        out[2].reshape(hid_size),
        out[3].T,
        out[4].T,
        out[5].reshape(256)[:classes],
    )


def solution(mesh):
    in_specs = (
        P(("row", "col"), None),
        P("row", "col", None, None, None),
        P("row", "col", None),
        P("row", "col", None),
        P(("row", "col")),
        P(("row", "col")),
        P(),
        P(),
        P(),
        P(),
        P(),
        P(),
    )
    out_specs = (P(), P(), P(), P(), P(), P())
    return jax.shard_map(
        on_device, mesh=mesh, in_specs=in_specs, out_specs=out_specs, check_vma=False
    )
```

```python
import functools
import math

import jax
import jax.numpy as jnp
from jax import lax
from jax.experimental import pallas as pl
from jax.experimental.pallas import tpu as pltpu
from jax.sharding import PartitionSpec as P

EDGE = 128
GROUP = 32
PAD = 176
NY, NZ = 4, 8
F32, BF16 = jnp.float32, jnp.bfloat16
VMEM = pl.BlockSpec(memory_space=pltpu.VMEM)
SMEM = pl.BlockSpec(memory_space=pltpu.SMEM)
ANY = pl.BlockSpec(memory_space=pl.ANY)
HBM = pl.BlockSpec(memory_space=pltpu.HBM)
NT = (((1,), (1,)), ((), ()))


def dot(a, b):
    return jnp.dot(a, b, preferred_element_type=F32)


def dot_nt(a, b):
    return lax.dot_general(a, b, NT, preferred_element_type=F32)


def call(body, out, specs, scratch=(), mib=4, flops=0, bytes_accessed=0):
    return pl.pallas_call(
        body,
        out_shape=out,
        in_specs=specs,
        out_specs=jax.tree.map(lambda _: VMEM, out),
        scratch_shapes=list(scratch),
        compiler_params=pltpu.CompilerParams(vmem_limit_bytes=mib * 1024 * 1024),
        cost_estimate=pl.CostEstimate(
            flops=flops, bytes_accessed=bytes_accessed, transcendentals=0
        ),
    )


def step(x, groups, shift):
    pairs = [(g[i], g[(i + shift) % len(g)]) for g in groups for i in range(len(g))]
    return lax.ppermute(x, "row", pairs)


ALONG_Z = [[NZ * y + z for z in range(NZ)] for y in range(NY)]
ALONG_Y = [[NZ * y + z for y in range(NY)] for z in range(NZ)]


def ring(x, groups):
    count = len(groups[0])
    up = down = x
    parts = [x]
    for _ in range(count // 2 - 1):
        up, down = step(up, groups, 1), step(down, groups, -1)
        parts += [up, down]
    half = x.shape[0] // 2
    return parts + [step(up[:half], groups, 1), step(down[half:], groups, -1)]


def along_y(x):
    return [x, step(x, ALONG_Y, 1), step(x, ALONG_Y, -1), step(x, ALONG_Y, 2)]


def place_of(block, row):
    owner = block // 2
    dz = (owner % NZ + NZ - row % NZ) % NZ
    dy = (owner // NZ + NY - row // NZ) % NY
    z_place = jnp.where(dz <= 3, 2 * dz, jnp.where(dz == 4, 7, 15 - 2 * dz))
    y_place = jnp.where(dy == 0, 0, jnp.where(dy == 3, 1, dy + 1))
    return z_place * NY + y_place


def slot_of(block, col):
    owner = block // 2
    dx = (owner // 2 + 4 - col // 2) % 4
    dc = (owner + col) % 2
    return (dc * 4 + dx) * 2 + block % 2


def to_sibling(x):
    return lax.ppermute(x, "col", [(i, i ^ 1) for i in range(8)])


def along_x(x, shift):
    return lax.ppermute(x, "col", [(i, (i + 2 * shift) % 8) for i in range(8)])


def start_parts(parts, held, sems):
    copies, at = [], 0
    for i, p in enumerate(parts):
        n = p.shape[0]
        copies.append(pltpu.make_async_copy(p, held.at[pl.ds(at, n)], sems.at[i]))
        copies[-1].start()
        at += n
    return copies


def start_pairs(feat_parts, agg_parts, held, sems):
    copies, at = [], 0
    for i, pair in enumerate(zip(feat_parts, agg_parts)):
        n = pair[0].shape[0]
        for j, p in enumerate(pair):
            to = held.at[pl.ds(at, n), :, pl.ds(j * EDGE, EDGE)]
            copies.append(pltpu.make_async_copy(p, to, sems.at[2 * i + j]))
            copies[-1].start()
        at += n
    return copies


def start_tiles(tiles, held, sems):
    copies = []
    for i in range(held.shape[0] // GROUP):
        at = pl.ds(i * GROUP, GROUP)
        copies.append(pltpu.make_async_copy(tiles.at[at], held.at[at], sems.at[i]))
        copies[-1].start()
    return copies


def start_all(pairs, sems):
    copies = [pltpu.make_async_copy(a, b, sems.at[i]) for i, (a, b) in enumerate(pairs)]
    for c in copies:
        c.start()
    return copies


def accumulate(tiles, held, sems, product, add):
    def body(i, carry):
        at = pl.ds(i * GROUP, GROUP)
        pltpu.make_async_copy(tiles.at[at], held.at[at], sems.at[i]).wait()
        got = [product(i * GROUP + u) for u in range(GROUP)]
        for u in range(GROUP):
            add(i * GROUP + u, got[u])
        return carry

    lax.fori_loop(0, held.shape[0] // GROUP, body, 0)


def degree_kernel(first, slots, tiles, out, held, sem):
    tiles = tiles.at[pl.ds(first, GROUP)]
    start_tiles(tiles, held, sem)
    out[...] = jnp.zeros_like(out)
    ones = jnp.ones((8, EDGE), BF16)

    def product(t):
        x = held[t].astype(F32)
        x = x * x
        hi = x.astype(BF16)
        lo = (x - hi.astype(F32)).astype(BF16)
        return dot_nt(ones, hi) + dot_nt(ones, lo)

    def add(t, got):
        out[slots[first + t]] += got

    accumulate(tiles, held, sem, product, add)


def first_kernel(n_parts, offs, cols, tiles_hbm, d0, d1, d2, d3, *refs):
    parts, keep, send, tiles, held, acc, tile_sem, sem = refs[:n_parts], *refs[n_parts:]
    copies = start_parts(parts, held, sem)
    start_tiles(tiles_hbm, tiles, tile_sem)
    acc[...] = jnp.zeros_like(acc)
    for s in range(16):
        deg = (d0[s][:1] + d1[s][:1]) + (d2[s][:1] + d3[s][:1])
        acc[pl.ds(s // 2 * 264 + 256 + s % 2, 1), :] = deg
    for c in copies:
        c.wait()

    def add(t, got):
        acc[pl.ds(pl.multiple_of(offs[t], 8), EDGE), :] += got

    accumulate(tiles_hbm, tiles, tile_sem, lambda t: dot(tiles[t], held[cols[t]]), add)
    keep[...] = acc[pl.ds(0, 1056), :]
    send[...] = acc[pl.ds(1056, 1056), :]


def join_first_kernel(keep, got, *out):
    for x in range(4):
        at = pl.ds(x * 264, 264)
        out[x][...] = keep[at, :] + got[at, :]


def flip(x):
    return x.astype(F32).T


def flip(x):
    return x.astype(F32).T


def pre_first(weights_t, bias_t, both):
    return dot_nt(weights_t, both) + bias_t


def aggregate_kernel(s0, s1, s2, s3, agg, inv):
    total = (s0[...] + s1[...]) + (s2[...] + s3[...])
    for b in range(2):
        x = 1.0 + total[256 + b : 257 + b]
        r = lax.rsqrt(x)
        r = r * (1.5 - 0.5 * x * r * r)
        inv[pl.ds(b, 1), :] = r
        column = jnp.broadcast_to(r, (EDGE, EDGE)).T
        agg[b] = (column * total[b * EDGE : (b + 1) * EDGE]).astype(BF16)


def second_kernel(n_parts, slots, cols, tiles_hbm, neigh_hbm, weights, bias, *refs):
    feat_parts, agg_parts = refs[:n_parts], refs[n_parts : 2 * n_parts]
    agg, keep, send, mine, tiles, neigh, both, held, acc, tile_sem, sem, neigh_sem = refs[2 * n_parts :]
    copies = start_pairs(feat_parts, agg_parts, both, sem)
    start_tiles(tiles_hbm, tiles, tile_sem)
    neigh_copy = pltpu.make_async_copy(neigh_hbm, neigh, neigh_sem)
    neigh_copy.start()
    acc[...] = jnp.zeros_like(acc)
    weights_t = flip(weights[...]).astype(BF16)
    wide = 4
    bias_t = jnp.broadcast_to(bias[...], (wide * EDGE, bias.shape[1])).T
    for c in copies:
        c.wait()

    def hidden(i, carry):
        x = both[pl.ds(i * wide, wide)].reshape(wide * EDGE, 2 * EDGE)
        h = jnp.maximum(pre_first(weights_t, bias_t, x), 0.0).astype(BF16)
        for q in range(wide):
            held[i * wide + q] = h[:, q * EDGE : (q + 1) * EDGE]
        return carry

    lax.fori_loop(0, 64 // wide, hidden, 0, unroll=2)
    mine[...] = held[pl.ds(0, 2)]

    def add(t, got):
        acc[slots[t]] += got

    accumulate(tiles_hbm, tiles, tile_sem, lambda t: dot_nt(held[cols[t]], tiles[t]), add)
    neigh_copy.wait()
    for s in range(16):
        agg[s] = acc[s].astype(BF16)
        got = dot(neigh[pl.ds(0, PAD), :], agg[s]).astype(BF16)
        if s < 8:
            keep[s] = got
        else:
            send[s - 8] = got


def join_second_kernel(keep, got, *out):
    for s in range(8):
        out[s // 2][s % 2] = (keep[s].astype(F32) + got[s].astype(F32)).astype(BF16)


def loss_kernel(
    classes, scale, s0, s1, s2, s3, hid, self_t, bias, labels, mask, inv, lg, w, grad, grad_bias
):
    rows = lax.broadcasted_iota(jnp.int32, (PAD, EDGE), 0)
    ones = jnp.ones((8, EDGE), BF16)
    for b in range(2):
        total = (s0[b].astype(F32) + s1[b].astype(F32)) + (s2[b].astype(F32) + s3[b].astype(F32))
        factor = inv[b : b + 1]
        logits = dot(self_t[pl.ds(0, PAD), :], hid[b]) + factor * total + bias[...]
        logits = jnp.where(rows < classes, logits, -1e30)
        e = jnp.exp(logits - jnp.max(logits, axis=0, keepdims=True))
        p = e / jnp.sum(e, axis=0, keepdims=True)
        p = p - jnp.where(rows == labels[b : b + 1], 1.0, 0.0)
        got = (p * (mask[b : b + 1].astype(F32) * scale)).astype(BF16)
        lg[b] = got
        w[b] = (got.astype(F32) * factor).astype(BF16)
        if b == 0:
            grad[...] = dot_nt(got, hid[b])
            grad_bias[...] = dot_nt(ones, got)
        else:
            grad[...] += dot_nt(got, hid[b])
            grad_bias[...] += dot_nt(ones, got)


X_ORDER = (0, 3, 1, 2)


def last_kernel(
    n_parts, slots, cols, w0, w1, w2, w3, weights, bias, tiles_hbm, agg_second_hbm, lg_hbm, self_hbm,
    neigh_hbm, grad_self_hbm, grad_bias, *refs
):
    feat_parts, agg_parts = refs[:n_parts], refs[n_parts : 2 * n_parts]
    (
        out, tiles, agg_second, lg, self_t, neigh_t, grad_self, both, acc, proj,
        tile_sem, both_sem, sems,
    ) = refs[2 * n_parts :]
    pairs = (
        (neigh_hbm, neigh_t),
        (agg_second_hbm, agg_second),
        (lg_hbm, lg),
        (self_hbm, self_t),
        (grad_self_hbm, grad_self),
    )
    small = start_all(pairs, sems)
    start_tiles(tiles_hbm, tiles, tile_sem)
    copies = start_pairs(feat_parts, agg_parts, both, both_sem)
    acc[...] = jnp.zeros_like(acc)
    weights_t = flip(weights[...]).astype(BF16)
    for c in small:
        c.wait()
    lacking = jnp.zeros((256 - PAD, EDGE), BF16)
    self_second = flip(self_t[...]).astype(BF16)
    neigh_second = flip(neigh_t[...]).astype(BF16)
    for b in range(2):
        acc[b] = dot(self_second, jnp.concatenate([lg[b], lacking], axis=0))
    g_neigh = jnp.zeros((PAD, 256), F32)
    for dx, part in zip(X_ORDER, (w0, w1, w2, w3)):
        at = [(i // 2 * 4 + dx) * 2 + i % 2 for i in range(4)]
        w = jnp.concatenate([part[i] for i in range(4)], axis=1)
        tall = jnp.concatenate([w, jnp.concatenate([lacking] * 4, axis=1)], axis=0)
        got = dot(neigh_second, tall).astype(BF16)
        for i in range(4):
            proj[at[i]] = got[:, i * EDGE : (i + 1) * EDGE]
        g_neigh += dot_nt(w, jnp.concatenate([agg_second[s] for s in at], axis=1))
    for i in range(2):
        lanes = slice(i * EDGE, (i + 1) * EDGE)
        out[pl.ds(512 + i * PAD, PAD), :] = grad_self[:, lanes].astype(BF16)
        out[pl.ds(512 + (2 + i) * PAD, PAD), :] = g_neigh[:, lanes].astype(BF16)

    def add(t, got):
        acc[cols[t]] += got

    accumulate(tiles_hbm, tiles, tile_sem, lambda t: dot(proj[slots[t]], tiles[t]), add)
    for c in copies:
        c.wait()
    wide = 8
    ones = jnp.ones((8, wide * EDGE), BF16)
    bias_t = jnp.broadcast_to(bias[...], (wide * EDGE, bias.shape[1])).T

    def contract(i, carry):
        g_first, g_bias = carry
        x = both[pl.ds(i * wide, wide)].reshape(wide * EDGE, 2 * EDGE)
        back = jnp.concatenate([acc[i * wide + q] for q in range(wide)], axis=1)
        p = jnp.where(pre_first(weights_t, bias_t, x) > 0.0, back, 0.0).astype(BF16)
        return g_first + dot(p, x), g_bias + dot_nt(ones, p)

    zeros = (jnp.zeros((256, 256), F32), jnp.zeros((8, 256), F32))
    g_first, g_bias = lax.fori_loop(0, 64 // wide, contract, zeros)
    out[pl.ds(0, 256), :] = g_first[:, :EDGE].astype(BF16)
    out[pl.ds(256, 256), :] = g_first[:, EDGE:].astype(BF16)
    pick = lax.broadcasted_iota(jnp.int32, (16, EDGE), 0)
    second = jnp.concatenate([grad_bias[:1], jnp.zeros((1, 256 - PAD), F32)], axis=1)
    rows = (g_bias[:1, :EDGE], g_bias[:1, EDGE:], second[:, :EDGE], second[:, EDGE:])
    last = jnp.zeros((16, EDGE), F32)
    for i, row in enumerate(rows):
        last = jnp.where(pick == i, row, last)
    end = 512 + 4 * PAD
    out[pl.ds(end, 16), :] = last.astype(BF16)
    out[pl.ds(end + 16, 1280 - 16 - end), :] = jnp.zeros((1280 - 16 - end, EDGE), BF16)


def add_pieces_kernel(x, out):
    total = x[0].astype(F32)
    for i in range(1, x.shape[0]):
        total = total + x[i].astype(F32)
    out[...] = total.astype(BF16)


def spread_kernel(a, b, out):
    total = (a[...].astype(F32) + b[...].astype(F32)).astype(BF16)
    for i in range(out.shape[0]):
        out[i] = total


def unpack_kernel(classes, x, self_first, neigh_first, bias_first, self_t, neigh_t, bias_second):
    self_first[...] = flip(x[pl.ds(0, 256), :])
    neigh_first[...] = flip(x[pl.ds(256, 256), :])
    for at, out in ((512, self_t), (512 + 2 * PAD, neigh_t)):
        for i in range(2):
            got = x[pl.ds(at + i * PAD, PAD), :].astype(F32)
            out[:, i * EDGE : (i + 1) * EDGE] = got[:classes]
    last = x[pl.ds(512 + 4 * PAD, 16), :].astype(F32)
    bias_first[...] = jnp.concatenate([last[0:1], last[1:2]], axis=1)
    bias_second[...] = jnp.concatenate([last[2:3], last[3:4]], axis=1)


def sum_everywhere(x):
    every = ("row", "col")
    number = lambda y, z, x, c: ((y * NZ + z) * 4 + x) * 2 + c
    groups = [
        [number(y, z, x, c) for y in range(NY) for x in range(4)] for z in range(NZ) for c in range(2)
    ]
    x = x.reshape(16, -1, EDGE)
    piece = jax.ShapeDtypeStruct(x.shape[1:], BF16)
    x = lax.all_to_all(x, every, 0, 0, tiled=True, axis_index_groups=groups)
    x = call(add_pieces_kernel, piece, [VMEM])(x)
    x = jnp.broadcast_to(x[None], (NZ,) + x.shape)
    x = lax.all_to_all(x, "row", 0, 0, tiled=True, axis_index_groups=ALONG_Z)
    x = call(add_pieces_kernel, piece, [VMEM])(x)
    x = call(spread_kernel, jax.ShapeDtypeStruct((16, 80, EDGE), BF16), [VMEM] * 2)(x, to_sibling(x))
    x = lax.all_to_all(x, every, 0, 0, tiled=True, axis_index_groups=groups)
    return x.reshape(-1, EDGE)


def on_device(
    features,
    tiles,
    block_rows,
    block_cols,
    labels,
    train_mask,
    self_first,
    neigh_first,
    bias_first,
    self_second,
    neigh_second,
    bias_second,
):
    classes = self_second.shape[1]
    hid_size = self_first.shape[1]
    scale = 1.0 / math.sqrt(65536)
    row, col = lax.axis_index("row"), lax.axis_index("col")
    tiles = tiles.reshape(-1, EDGE, EDGE)
    slots = slot_of(block_rows.reshape(-1), col)
    sources = block_cols.reshape(-1)
    cols = place_of(sources, row) * 2 + sources % 2
    offs = slots // 2 * 264 + slots % 2 * EDGE
    shape = jax.ShapeDtypeStruct
    dma = pltpu.SemaphoreType.DMA
    feat = features.reshape(2, EDGE, EDGE)
    tile_buffer = pltpu.VMEM(tiles.shape, BF16)
    n_groups = tiles.shape[0] // GROUP

    feat_parts = ring(jnp.concatenate(along_y(feat), axis=0), ALONG_Z)
    n_feat = len(feat_parts)
    degs = [
        call(
            functools.partial(degree_kernel, i * GROUP),
            shape((16, 8, EDGE), F32),
            [SMEM, HBM],
            [pltpu.VMEM((GROUP, EDGE, EDGE), BF16), dma((1,))],
            mib=60,
            flops=2**32,
            bytes_accessed=2**20,
        )(slots, tiles)
        for i in range(n_groups)
    ]
    block = shape((1056, EDGE), F32)
    keep, send = call(
        functools.partial(first_kernel, n_feat),
        (block, block),
        [SMEM, SMEM, HBM] + [VMEM] * 4 + [ANY] * n_feat,
        [
            tile_buffer,
            pltpu.VMEM((64, EDGE, EDGE), BF16),
            pltpu.VMEM((2112, EDGE), F32),
            dma((n_groups,)),
            dma((n_feat,)),
        ],
        mib=60,
        flops=2**29,
        bytes_accessed=2**23,
    )(offs, cols, tiles, *degs, *feat_parts)
    sums = call(join_first_kernel, (shape((264, EDGE), F32),) * 4, [VMEM] * 2)(
        keep, to_sibling(send)
    )
    agg, inv = call(
        aggregate_kernel, (shape((2, EDGE, EDGE), BF16), shape((2, EDGE), F32)), [VMEM] * 4
    )(sums[0], along_x(sums[1], 1), along_x(sums[2], 2), along_x(sums[3], 3))
    agg_parts = ring(jnp.concatenate(along_y(agg), axis=0), ALONG_Z)
    weights = jnp.concatenate([self_first, neigh_first], axis=0)
    bias = bias_first.reshape(1, -1)

    lacking = ((0, 256 - classes), (0, 0))
    self_t = jnp.pad(self_second.T, lacking)
    neigh_t = jnp.pad(neigh_second.T, lacking)
    bias_wide = jnp.broadcast_to(jnp.pad(bias_second, (0, PAD - classes))[:, None], (PAD, EDGE))
    half = shape((8, PAD, EDGE), BF16)
    agg_second, keep, send, hid = call(
        functools.partial(second_kernel, n_feat),
        (shape((16, hid_size, EDGE), BF16), half, half, shape((2, hid_size, EDGE), BF16)),
        [SMEM, SMEM, HBM, HBM, VMEM, VMEM] + [HBM] * (2 * n_feat),
        [
            tile_buffer,
            pltpu.VMEM((256, hid_size), BF16),
            pltpu.VMEM((64, EDGE, 2 * EDGE), BF16),
            pltpu.VMEM((64, hid_size, EDGE), BF16),
            pltpu.VMEM((16, hid_size, EDGE), F32),
            dma((n_groups,)),
            dma((2 * n_feat,)),
            dma(()),
        ],
        mib=60,
        flops=2**31,
        bytes_accessed=2**23,
    )(slots, cols, tiles, neigh_t, weights, bias, *feat_parts, *agg_parts)
    sums = call(join_second_kernel, (shape((2, PAD, EDGE), BF16),) * 4, [VMEM] * 2)(
        keep, to_sibling(send)
    )
    lg, w, grad_self, grad_bias = call(
        functools.partial(loss_kernel, classes, scale),
        (
            shape((2, PAD, EDGE), BF16),
            shape((2, PAD, EDGE), BF16),
            shape((PAD, hid_size), F32),
            shape((8, PAD), F32),
        ),
        [VMEM] * 10,
    )(
        sums[0],
        along_x(sums[1], 1),
        along_x(sums[2], 2),
        along_x(sums[3], 3),
        hid,
        self_t,
        bias_wide,
        labels.reshape(2, EDGE),
        train_mask.reshape(2, EDGE),
        inv,
    )
    w = jnp.concatenate([w, to_sibling(w)], axis=0)
    w_parts = [w, along_x(w, 1), along_x(w, 3), along_x(w, 2)]
    grads = call(
        functools.partial(last_kernel, n_feat),
        shape((1280, EDGE), BF16),
        [SMEM] * 2 + [VMEM] * 6 + [HBM] * 6 + [VMEM] + [HBM] * (2 * n_feat),
        [
            tile_buffer,
            pltpu.VMEM((16, hid_size, EDGE), BF16),
            pltpu.VMEM((2, PAD, EDGE), BF16),
            pltpu.VMEM((256, hid_size), BF16),
            pltpu.VMEM((256, hid_size), BF16),
            pltpu.VMEM((PAD, hid_size), F32),
            pltpu.VMEM((64, EDGE, 2 * EDGE), BF16),
            pltpu.VMEM((64, hid_size, EDGE), F32),
            pltpu.VMEM((16, hid_size, EDGE), BF16),
            dma((n_groups,)),
            dma((2 * n_feat,)),
            dma((5,)),
        ],
        mib=60,
        flops=2**31,
        bytes_accessed=2**24,
    )(
        slots, cols, *w_parts, weights, bias, tiles, agg_second, lg, self_t, neigh_t, grad_self,
        grad_bias, *feat_parts, *agg_parts
    )
    out = call(
        functools.partial(unpack_kernel, classes),
        (
            shape(self_first.shape, F32),
            shape(neigh_first.shape, F32),
            shape((1, hid_size), F32),
            shape((classes, hid_size), F32),
            shape((classes, hid_size), F32),
            shape((1, 256), F32),
        ),
        [VMEM],
    )(sum_everywhere(grads))
    return (
        out[0],
        out[1],
        out[2].reshape(hid_size),
        out[3].T,
        out[4].T,
        out[5].reshape(256)[:classes],
    )


def solution(mesh):
    in_specs = (
        P(("row", "col"), None),
        P("row", "col", None, None, None),
        P("row", "col", None),
        P("row", "col", None),
        P(("row", "col")),
        P(("row", "col")),
        P(),
        P(),
        P(),
        P(),
        P(),
        P(),
    )
    out_specs = (P(), P(), P(), P(), P(), P())
    return jax.shard_map(
        on_device, mesh=mesh, in_specs=in_specs, out_specs=out_specs, check_vma=False
    )
```

```python
import functools
import math

import jax
import jax.numpy as jnp
from jax import lax
from jax.experimental import pallas as pl
from jax.experimental.pallas import tpu as pltpu
from jax.sharding import PartitionSpec as P

EDGE = 128
GROUP = 32
PAD = 176
NY, NZ = 4, 8
F32, BF16 = jnp.float32, jnp.bfloat16
VMEM = pl.BlockSpec(memory_space=pltpu.VMEM)
SMEM = pl.BlockSpec(memory_space=pltpu.SMEM)
ANY = pl.BlockSpec(memory_space=pl.ANY)
NT = (((1,), (1,)), ((), ()))


def dot(a, b):
    return jnp.dot(a, b, preferred_element_type=F32)


def dot_nt(a, b):
    return lax.dot_general(a, b, NT, preferred_element_type=F32)


def call(body, out, specs, scratch=(), mib=4, flops=0, bytes_accessed=0):
    return pl.pallas_call(
        body,
        out_shape=out,
        in_specs=specs,
        out_specs=jax.tree.map(lambda _: VMEM, out),
        scratch_shapes=list(scratch),
        compiler_params=pltpu.CompilerParams(vmem_limit_bytes=mib * 1024 * 1024),
        cost_estimate=pl.CostEstimate(
            flops=flops, bytes_accessed=bytes_accessed, transcendentals=0
        ),
    )


def step(x, groups, shift):
    pairs = [(g[i], g[(i + shift) % len(g)]) for g in groups for i in range(len(g))]
    return lax.ppermute(x, "row", pairs)


ALONG_Z = [[NZ * y + z for z in range(NZ)] for y in range(NY)]
ALONG_Y = [[NZ * y + z for y in range(NY)] for z in range(NZ)]


def ring(x, groups):
    count = len(groups[0])
    up = down = x
    parts = [x]
    for _ in range(count // 2 - 1):
        up, down = step(up, groups, 1), step(down, groups, -1)
        parts += [up, down]
    half = x.shape[0] // 2
    return parts + [step(up[:half], groups, 1), step(down[half:], groups, -1)]


def along_y(x):
    return [x, step(x, ALONG_Y, 1), step(x, ALONG_Y, -1), step(x, ALONG_Y, 2)]


def place_of(block, row):
    owner = block // 2
    dz = (owner % NZ + NZ - row % NZ) % NZ
    dy = (owner // NZ + NY - row // NZ) % NY
    z_place = jnp.where(dz <= 3, 2 * dz, jnp.where(dz == 4, 7, 15 - 2 * dz))
    y_place = jnp.where(dy == 0, 0, jnp.where(dy == 3, 1, dy + 1))
    return z_place * NY + y_place


def slot_of(block, col):
    owner = block // 2
    dx = (owner // 2 + 4 - col // 2) % 4
    dc = (owner + col) % 2
    return (dc * 4 + dx) * 2 + block % 2


def to_sibling(x):
    return lax.ppermute(x, "col", [(i, i ^ 1) for i in range(8)])


def along_x(x, shift):
    return lax.ppermute(x, "col", [(i, (i + 2 * shift) % 8) for i in range(8)])


def start_parts(parts, held, sems):
    copies, at = [], 0
    for i, p in enumerate(parts):
        n = p.shape[0]
        copies.append(pltpu.make_async_copy(p, held.at[pl.ds(at, n)], sems.at[i]))
        copies[-1].start()
        at += n
    return copies


def start_pairs(feat_parts, agg_parts, held, sems):
    copies, at = [], 0
    for i, pair in enumerate(zip(feat_parts, agg_parts)):
        n = pair[0].shape[0]
        for j, p in enumerate(pair):
            to = held.at[pl.ds(at, n), :, pl.ds(j * EDGE, EDGE)]
            copies.append(pltpu.make_async_copy(p, to, sems.at[2 * i + j]))
            copies[-1].start()
        at += n
    return copies


def accumulate(count, product, add):
    def body(i, carry):
        got = [product(i * GROUP + u) for u in range(GROUP)]
        for u in range(GROUP):
            add(i * GROUP + u, got[u])
        return carry

    lax.fori_loop(0, count // GROUP, body, 0)


def degree_kernel(first, slots, tiles, out):
    out[...] = jnp.zeros_like(out)
    ones = jnp.ones((8, EDGE), BF16)

    def product(t):
        x = tiles[first + t].astype(F32)
        x = x * x
        hi = x.astype(BF16)
        lo = (x - hi.astype(F32)).astype(BF16)
        return dot_nt(ones, hi) + dot_nt(ones, lo)

    def add(t, got):
        out[slots[first + t]] += got

    accumulate(GROUP, product, add)


def first_kernel(n_parts, offs, cols, tiles, d0, d1, d2, d3, *refs):
    parts, keep, send, held, acc, sem = refs[:n_parts], *refs[n_parts:]
    copies = start_parts(parts, held, sem)
    acc[...] = jnp.zeros_like(acc)
    for s in range(16):
        deg = (d0[s][:1] + d1[s][:1]) + (d2[s][:1] + d3[s][:1])
        acc[pl.ds(s // 2 * 264 + 256 + s % 2, 1), :] = deg
    for c in copies:
        c.wait()

    def add(t, got):
        acc[pl.ds(pl.multiple_of(offs[t], 8), EDGE), :] += got

    accumulate(tiles.shape[0], lambda t: dot(tiles[t], held[cols[t]]), add)
    keep[...] = acc[pl.ds(0, 1056), :]
    send[...] = acc[pl.ds(1056, 1056), :]


def join_first_kernel(keep, got, *out):
    for x in range(4):
        at = pl.ds(x * 264, 264)
        out[x][...] = keep[at, :] + got[at, :]


def flip(x):
    return x.astype(F32).T


def flip(x):
    return x.astype(F32).T


def pre_first(weights_t, bias_t, both):
    return dot_nt(weights_t, both) + bias_t


def aggregate_kernel(s0, s1, s2, s3, agg, inv):
    total = (s0[...] + s1[...]) + (s2[...] + s3[...])
    for b in range(2):
        x = 1.0 + total[256 + b : 257 + b]
        r = lax.rsqrt(x)
        r = r * (1.5 - 0.5 * x * r * r)
        inv[pl.ds(b, 1), :] = r
        column = jnp.broadcast_to(r, (EDGE, EDGE)).T
        agg[b] = (column * total[b * EDGE : (b + 1) * EDGE]).astype(BF16)


def second_kernel(n_parts, slots, cols, tiles, neigh, weights, bias, *refs):
    feat_parts, agg_parts = refs[:n_parts], refs[n_parts : 2 * n_parts]
    agg, keep, send, mine, both, held, acc, sem = refs[2 * n_parts :]
    copies = start_pairs(feat_parts, agg_parts, both, sem)
    acc[...] = jnp.zeros_like(acc)
    weights_t = flip(weights[...]).astype(BF16)
    wide = 4
    bias_t = jnp.broadcast_to(bias[...], (wide * EDGE, bias.shape[1])).T
    for c in copies:
        c.wait()

    def hidden(i, carry):
        x = both[pl.ds(i * wide, wide)].reshape(wide * EDGE, 2 * EDGE)
        h = jnp.maximum(pre_first(weights_t, bias_t, x), 0.0).astype(BF16)
        for q in range(wide):
            held[i * wide + q] = h[:, q * EDGE : (q + 1) * EDGE]
        return carry

    lax.fori_loop(0, 64 // wide, hidden, 0, unroll=2)
    mine[...] = held[pl.ds(0, 2)]

    def add(t, got):
        acc[slots[t]] += got

    accumulate(tiles.shape[0], lambda t: dot_nt(held[cols[t]], tiles[t]), add)
    for s in range(16):
        agg[s] = acc[s].astype(BF16)
        got = dot(neigh[pl.ds(0, PAD), :], agg[s]).astype(BF16)
        if s < 8:
            keep[s] = got
        else:
            send[s - 8] = got


def join_second_kernel(keep, got, *out):
    for s in range(8):
        out[s // 2][s % 2] = (keep[s].astype(F32) + got[s].astype(F32)).astype(BF16)


def loss_kernel(
    classes, scale, s0, s1, s2, s3, hid, self_t, bias, labels, mask, inv, lg, w, grad, grad_bias
):
    rows = lax.broadcasted_iota(jnp.int32, (PAD, EDGE), 0)
    ones = jnp.ones((8, EDGE), BF16)
    for b in range(2):
        total = (s0[b].astype(F32) + s1[b].astype(F32)) + (s2[b].astype(F32) + s3[b].astype(F32))
        factor = inv[b : b + 1]
        logits = dot(self_t[pl.ds(0, PAD), :], hid[b]) + factor * total + bias[...]
        logits = jnp.where(rows < classes, logits, -1e30)
        e = jnp.exp(logits - jnp.max(logits, axis=0, keepdims=True))
        p = e / jnp.sum(e, axis=0, keepdims=True)
        p = p - jnp.where(rows == labels[b : b + 1], 1.0, 0.0)
        got = (p * (mask[b : b + 1].astype(F32) * scale)).astype(BF16)
        lg[b] = got
        w[b] = (got.astype(F32) * factor).astype(BF16)
        if b == 0:
            grad[...] = dot_nt(got, hid[b])
            grad_bias[...] = dot_nt(ones, got)
        else:
            grad[...] += dot_nt(got, hid[b])
            grad_bias[...] += dot_nt(ones, got)


X_ORDER = (0, 3, 1, 2)


def last_kernel(
    n_parts, slots, cols, w0, w1, w2, w3, weights, bias, tiles, agg_second, lg, self_t, neigh_t,
    grad_self, grad_bias, *refs
):
    feat_parts, agg_parts = refs[:n_parts], refs[n_parts : 2 * n_parts]
    out, both, acc, proj, both_sem = refs[2 * n_parts :]
    copies = start_pairs(feat_parts, agg_parts, both, both_sem)
    acc[...] = jnp.zeros_like(acc)
    weights_t = flip(weights[...]).astype(BF16)
    lacking = jnp.zeros((256 - PAD, EDGE), BF16)
    self_second = flip(self_t[...]).astype(BF16)
    neigh_second = flip(neigh_t[...]).astype(BF16)
    for b in range(2):
        acc[b] = dot(self_second, jnp.concatenate([lg[b], lacking], axis=0))
    g_neigh = jnp.zeros((PAD, 256), F32)
    for dx, part in zip(X_ORDER, (w0, w1, w2, w3)):
        at = [(i // 2 * 4 + dx) * 2 + i % 2 for i in range(4)]
        w = jnp.concatenate([part[i] for i in range(4)], axis=1)
        tall = jnp.concatenate([w, jnp.concatenate([lacking] * 4, axis=1)], axis=0)
        got = dot(neigh_second, tall).astype(BF16)
        for i in range(4):
            proj[at[i]] = got[:, i * EDGE : (i + 1) * EDGE]
        g_neigh += dot_nt(w, jnp.concatenate([agg_second[s] for s in at], axis=1))
    for i in range(2):
        lanes = slice(i * EDGE, (i + 1) * EDGE)
        out[pl.ds(512 + i * PAD, PAD), :] = grad_self[:, lanes].astype(BF16)
        out[pl.ds(512 + (2 + i) * PAD, PAD), :] = g_neigh[:, lanes].astype(BF16)

    def add(t, got):
        acc[cols[t]] += got

    accumulate(tiles.shape[0], lambda t: dot(proj[slots[t]], tiles[t]), add)
    for c in copies:
        c.wait()
    wide = 8
    ones = jnp.ones((8, wide * EDGE), BF16)
    bias_t = jnp.broadcast_to(bias[...], (wide * EDGE, bias.shape[1])).T

    def contract(i, carry):
        g_first, g_bias = carry
        x = both[pl.ds(i * wide, wide)].reshape(wide * EDGE, 2 * EDGE)
        back = jnp.concatenate([acc[i * wide + q] for q in range(wide)], axis=1)
        p = jnp.where(pre_first(weights_t, bias_t, x) > 0.0, back, 0.0).astype(BF16)
        return g_first + dot(p, x), g_bias + dot_nt(ones, p)

    zeros = (jnp.zeros((256, 256), F32), jnp.zeros((8, 256), F32))
    g_first, g_bias = lax.fori_loop(0, 64 // wide, contract, zeros)
    out[pl.ds(0, 256), :] = g_first[:, :EDGE].astype(BF16)
    out[pl.ds(256, 256), :] = g_first[:, EDGE:].astype(BF16)
    pick = lax.broadcasted_iota(jnp.int32, (16, EDGE), 0)
    second = jnp.concatenate([grad_bias[:1], jnp.zeros((1, 256 - PAD), F32)], axis=1)
    rows = (g_bias[:1, :EDGE], g_bias[:1, EDGE:], second[:, :EDGE], second[:, EDGE:])
    last = jnp.zeros((16, EDGE), F32)
    for i, row in enumerate(rows):
        last = jnp.where(pick == i, row, last)
    end = 512 + 4 * PAD
    out[pl.ds(end, 16), :] = last.astype(BF16)
    out[pl.ds(end + 16, 1280 - 16 - end), :] = jnp.zeros((1280 - 16 - end, EDGE), BF16)


def add_pieces_kernel(x, out):
    total = x[0].astype(F32)
    for i in range(1, x.shape[0]):
        total = total + x[i].astype(F32)
    out[...] = total.astype(BF16)


def spread_kernel(a, b, out):
    total = (a[...].astype(F32) + b[...].astype(F32)).astype(BF16)
    for i in range(out.shape[0]):
        out[i] = total


def unpack_kernel(classes, x, self_first, neigh_first, bias_first, self_t, neigh_t, bias_second):
    self_first[...] = flip(x[pl.ds(0, 256), :])
    neigh_first[...] = flip(x[pl.ds(256, 256), :])
    for at, out in ((512, self_t), (512 + 2 * PAD, neigh_t)):
        for i in range(2):
            got = x[pl.ds(at + i * PAD, PAD), :].astype(F32)
            out[:, i * EDGE : (i + 1) * EDGE] = got[:classes]
    last = x[pl.ds(512 + 4 * PAD, 16), :].astype(F32)
    bias_first[...] = jnp.concatenate([last[0:1], last[1:2]], axis=1)
    bias_second[...] = jnp.concatenate([last[2:3], last[3:4]], axis=1)


def sum_everywhere(x):
    every = ("row", "col")
    number = lambda y, z, x, c: ((y * NZ + z) * 4 + x) * 2 + c
    groups = [
        [number(y, z, x, c) for y in range(NY) for x in range(4)] for z in range(NZ) for c in range(2)
    ]
    x = x.reshape(16, -1, EDGE)
    piece = jax.ShapeDtypeStruct(x.shape[1:], BF16)
    x = lax.all_to_all(x, every, 0, 0, tiled=True, axis_index_groups=groups)
    x = call(add_pieces_kernel, piece, [VMEM])(x)
    x = jnp.broadcast_to(x[None], (NZ,) + x.shape)
    x = lax.all_to_all(x, "row", 0, 0, tiled=True, axis_index_groups=ALONG_Z)
    x = call(add_pieces_kernel, piece, [VMEM])(x)
    x = call(spread_kernel, jax.ShapeDtypeStruct((16, 80, EDGE), BF16), [VMEM] * 2)(x, to_sibling(x))
    x = lax.all_to_all(x, every, 0, 0, tiled=True, axis_index_groups=groups)
    return x.reshape(-1, EDGE)


def on_device(
    features,
    tiles,
    block_rows,
    block_cols,
    labels,
    train_mask,
    self_first,
    neigh_first,
    bias_first,
    self_second,
    neigh_second,
    bias_second,
):
    classes = self_second.shape[1]
    hid_size = self_first.shape[1]
    scale = 1.0 / math.sqrt(65536)
    row, col = lax.axis_index("row"), lax.axis_index("col")
    tiles = tiles.reshape(-1, EDGE, EDGE)
    slots = slot_of(block_rows.reshape(-1), col)
    sources = block_cols.reshape(-1)
    cols = place_of(sources, row) * 2 + sources % 2
    offs = slots // 2 * 264 + slots % 2 * EDGE
    shape = jax.ShapeDtypeStruct
    dma = pltpu.SemaphoreType.DMA
    feat = features.reshape(2, EDGE, EDGE)
    n_groups = tiles.shape[0] // GROUP

    feat_parts = ring(jnp.concatenate(along_y(feat), axis=0), ALONG_Z)
    n_feat = len(feat_parts)
    degs = [
        call(
            functools.partial(degree_kernel, i * GROUP),
            shape((16, 8, EDGE), F32),
            [SMEM, VMEM],
            mib=4,
            flops=2**32,
            bytes_accessed=2**20,
        )(slots, tiles)
        for i in range(n_groups)
    ]
    block = shape((1056, EDGE), F32)
    keep, send = call(
        functools.partial(first_kernel, n_feat),
        (block, block),
        [SMEM] * 2 + [VMEM] * 5 + [ANY] * n_feat,
        [
            pltpu.VMEM((64, EDGE, EDGE), BF16),
            pltpu.VMEM((2112, EDGE), F32),
            dma((n_feat,)),
        ],
        mib=8,
        flops=2**29,
        bytes_accessed=2**23,
    )(offs, cols, tiles, *degs, *feat_parts)
    sums = call(join_first_kernel, (shape((264, EDGE), F32),) * 4, [VMEM] * 2)(
        keep, to_sibling(send)
    )
    agg, inv = call(
        aggregate_kernel, (shape((2, EDGE, EDGE), BF16), shape((2, EDGE), F32)), [VMEM] * 4
    )(sums[0], along_x(sums[1], 1), along_x(sums[2], 2), along_x(sums[3], 3))
    agg_parts = ring(jnp.concatenate(along_y(agg), axis=0), ALONG_Z)
    weights = jnp.concatenate([self_first, neigh_first], axis=0)
    bias = bias_first.reshape(1, -1)

    lacking = ((0, 256 - classes), (0, 0))
    self_t = jnp.pad(self_second.T, lacking)
    neigh_t = jnp.pad(neigh_second.T, lacking)
    bias_wide = jnp.broadcast_to(jnp.pad(bias_second, (0, PAD - classes))[:, None], (PAD, EDGE))
    half = shape((8, PAD, EDGE), BF16)
    agg_second, keep, send, hid = call(
        functools.partial(second_kernel, n_feat),
        (shape((16, hid_size, EDGE), BF16), half, half, shape((2, hid_size, EDGE), BF16)),
        [SMEM] * 2 + [VMEM] * 4 + [ANY] * (2 * n_feat),
        [
            pltpu.VMEM((64, EDGE, 2 * EDGE), BF16),
            pltpu.VMEM((64, hid_size, EDGE), BF16),
            pltpu.VMEM((16, hid_size, EDGE), F32),
            dma((2 * n_feat,)),
        ],
        mib=18,
        flops=2**31,
        bytes_accessed=2**23,
    )(slots, cols, tiles, neigh_t, weights, bias, *feat_parts, *agg_parts)
    sums = call(join_second_kernel, (shape((2, PAD, EDGE), BF16),) * 4, [VMEM] * 2)(
        keep, to_sibling(send)
    )
    lg, w, grad_self, grad_bias = call(
        functools.partial(loss_kernel, classes, scale),
        (
            shape((2, PAD, EDGE), BF16),
            shape((2, PAD, EDGE), BF16),
            shape((PAD, hid_size), F32),
            shape((8, PAD), F32),
        ),
        [VMEM] * 10,
    )(
        sums[0],
        along_x(sums[1], 1),
        along_x(sums[2], 2),
        along_x(sums[3], 3),
        hid,
        self_t,
        bias_wide,
        labels.reshape(2, EDGE),
        train_mask.reshape(2, EDGE),
        inv,
    )
    w = jnp.concatenate([w, to_sibling(w)], axis=0)
    w_parts = [w, along_x(w, 1), along_x(w, 3), along_x(w, 2)]
    grads = call(
        functools.partial(last_kernel, n_feat),
        shape((1280, EDGE), BF16),
        [SMEM] * 2 + [VMEM] * 13 + [ANY] * (2 * n_feat),
        [
            pltpu.VMEM((64, EDGE, 2 * EDGE), BF16),
            pltpu.VMEM((64, hid_size, EDGE), F32),
            pltpu.VMEM((16, hid_size, EDGE), BF16),
            dma((2 * n_feat,)),
        ],
        mib=22,
        flops=2**31,
        bytes_accessed=2**24,
    )(
        slots, cols, *w_parts, weights, bias, tiles, agg_second, lg, self_t, neigh_t, grad_self,
        grad_bias, *feat_parts, *agg_parts
    )
    out = call(
        functools.partial(unpack_kernel, classes),
        (
            shape(self_first.shape, F32),
            shape(neigh_first.shape, F32),
            shape((1, hid_size), F32),
            shape((classes, hid_size), F32),
            shape((classes, hid_size), F32),
            shape((1, 256), F32),
        ),
        [VMEM],
    )(sum_everywhere(grads))
    return (
        out[0],
        out[1],
        out[2].reshape(hid_size),
        out[3].T,
        out[4].T,
        out[5].reshape(256)[:classes],
    )


def solution(mesh):
    in_specs = (
        P(("row", "col"), None),
        P("row", "col", None, None, None),
        P("row", "col", None),
        P("row", "col", None),
        P(("row", "col")),
        P(("row", "col")),
        P(),
        P(),
        P(),
        P(),
        P(),
        P(),
    )
    out_specs = (P(), P(), P(), P(), P(), P())
    return jax.shard_map(
        on_device, mesh=mesh, in_specs=in_specs, out_specs=out_specs, check_vma=False
    )
```

```python
import functools
import math

import jax
import jax.numpy as jnp
from jax import lax
from jax.experimental import pallas as pl
from jax.experimental.pallas import tpu as pltpu
from jax.sharding import PartitionSpec as P

EDGE = 128
GROUP = 32
PAD = 176
NY, NZ = 4, 8
F32, BF16 = jnp.float32, jnp.bfloat16
VMEM = pl.BlockSpec(memory_space=pltpu.VMEM)
SMEM = pl.BlockSpec(memory_space=pltpu.SMEM)
ANY = pl.BlockSpec(memory_space=pl.ANY)
NT = (((1,), (1,)), ((), ()))


def dot(a, b):
    return jnp.dot(a, b, preferred_element_type=F32)


def dot_nt(a, b):
    return lax.dot_general(a, b, NT, preferred_element_type=F32)


def call(body, out, specs, scratch=(), mib=4, flops=0, bytes_accessed=0):
    return pl.pallas_call(
        body,
        out_shape=out,
        in_specs=specs,
        out_specs=jax.tree.map(lambda _: VMEM, out),
        scratch_shapes=list(scratch),
        compiler_params=pltpu.CompilerParams(vmem_limit_bytes=mib * 1024 * 1024),
        cost_estimate=pl.CostEstimate(
            flops=flops, bytes_accessed=bytes_accessed, transcendentals=0
        ),
    )


def step(x, groups, shift):
    pairs = [(g[i], g[(i + shift) % len(g)]) for g in groups for i in range(len(g))]
    return lax.ppermute(x, "row", pairs)


ALONG_Z = [[NZ * y + z for z in range(NZ)] for y in range(NY)]
ALONG_Y = [[NZ * y + z for y in range(NY)] for z in range(NZ)]


def ring(x, groups):
    count = len(groups[0])
    up = down = x
    parts = [x]
    for _ in range(count // 2 - 1):
        up, down = step(up, groups, 1), step(down, groups, -1)
        parts += [up, down]
    half = x.shape[0] // 2
    return parts + [step(up[:half], groups, 1), step(down[half:], groups, -1)]


def along_y(x):
    return [x, step(x, ALONG_Y, 1), step(x, ALONG_Y, -1), step(x, ALONG_Y, 2)]


def place_of(block, row):
    owner = block // 2
    dz = (owner % NZ + NZ - row % NZ) % NZ
    dy = (owner // NZ + NY - row // NZ) % NY
    z_place = jnp.where(dz <= 3, 2 * dz, jnp.where(dz == 4, 7, 15 - 2 * dz))
    y_place = jnp.where(dy == 0, 0, jnp.where(dy == 3, 1, dy + 1))
    return z_place * NY + y_place


def slot_of(block, col):
    owner = block // 2
    dx = (owner // 2 + 4 - col // 2) % 4
    dc = (owner + col) % 2
    return (dc * 4 + dx) * 2 + block % 2


def to_sibling(x):
    return lax.ppermute(x, "col", [(i, i ^ 1) for i in range(8)])


def along_x(x, shift):
    return lax.ppermute(x, "col", [(i, (i + 2 * shift) % 8) for i in range(8)])


def start_parts(parts, held, sems):
    copies, at = [], 0
    for i, p in enumerate(parts):
        n = p.shape[0]
        copies.append(pltpu.make_async_copy(p, held.at[pl.ds(at, n)], sems.at[i]))
        copies[-1].start()
        at += n
    return copies


def start_pairs(feat_parts, agg_parts, held, sems):
    copies, at = [], 0
    for i, pair in enumerate(zip(feat_parts, agg_parts)):
        n = pair[0].shape[0]
        for j, p in enumerate(pair):
            to = held.at[pl.ds(at, n), :, pl.ds(j * EDGE, EDGE)]
            copies.append(pltpu.make_async_copy(p, to, sems.at[2 * i + j]))
            copies[-1].start()
        at += n
    return copies


def accumulate(count, product, add):
    def body(i, carry):
        got = [product(i * GROUP + u) for u in range(GROUP)]
        for u in range(GROUP):
            add(i * GROUP + u, got[u])
        return carry

    lax.fori_loop(0, count // GROUP, body, 0)


def degree_kernel(first, slots, tiles, out):
    out[...] = jnp.zeros_like(out)
    ones = jnp.ones((8, EDGE), BF16)

    def product(t):
        x = tiles[first + t].astype(F32)
        x = x * x
        hi = x.astype(BF16)
        lo = (x - hi.astype(F32)).astype(BF16)
        return dot_nt(ones, hi) + dot_nt(ones, lo)

    def add(t, got):
        out[slots[first + t]] += got

    accumulate(GROUP, product, add)


def first_kernel(n_parts, offs, cols, tiles, d0, d1, d2, d3, *refs):
    parts, keep, send, held, acc, sem = refs[:n_parts], *refs[n_parts:]
    copies = start_parts(parts, held, sem)
    acc[...] = jnp.zeros_like(acc)
    for s in range(16):
        deg = (d0[s][:1] + d1[s][:1]) + (d2[s][:1] + d3[s][:1])
        acc[pl.ds(s // 2 * 264 + 256 + s % 2, 1), :] = deg
    for c in copies:
        c.wait()

    def add(t, got):
        acc[pl.ds(pl.multiple_of(offs[t], 8), EDGE), :] += got

    accumulate(tiles.shape[0], lambda t: dot(tiles[t], held[cols[t]]), add)
    keep[...] = acc[pl.ds(0, 1056), :]
    send[...] = acc[pl.ds(1056, 1056), :]


def join_first_kernel(keep, got, *out):
    for x in range(4):
        at = pl.ds(x * 264, 264)
        out[x][...] = keep[at, :] + got[at, :]


def flip(x):
    return x.astype(F32).T


def flip(x):
    return x.astype(F32).T


def pre_first(weights_t, bias_t, both):
    return dot_nt(weights_t, both) + bias_t


def aggregate_kernel(s0, s1, s2, s3, agg, inv):
    total = (s0[...] + s1[...]) + (s2[...] + s3[...])
    for b in range(2):
        x = 1.0 + total[256 + b : 257 + b]
        r = lax.rsqrt(x)
        r = r * (1.5 - 0.5 * x * r * r)
        inv[pl.ds(b, 1), :] = r
        column = jnp.broadcast_to(r, (EDGE, EDGE)).T
        agg[b] = (column * total[b * EDGE : (b + 1) * EDGE]).astype(BF16)


def second_kernel(n_parts, slots, cols, tiles, neigh, weights, bias, *refs):
    feat_parts, agg_parts = refs[:n_parts], refs[n_parts : 2 * n_parts]
    agg, keep, send, mine, both, held, acc, sem = refs[2 * n_parts :]
    copies = start_pairs(feat_parts, agg_parts, both, sem)
    acc[...] = jnp.zeros_like(acc)
    weights_t = flip(weights[...]).astype(BF16)
    wide = 4
    bias_t = jnp.broadcast_to(bias[...], (wide * EDGE, bias.shape[1])).T
    for c in copies:
        c.wait()

    def hidden(i, carry):
        x = both[pl.ds(i * wide, wide)].reshape(wide * EDGE, 2 * EDGE)
        h = jnp.maximum(pre_first(weights_t, bias_t, x), 0.0).astype(BF16)
        for q in range(wide):
            held[i * wide + q] = h[:, q * EDGE : (q + 1) * EDGE]
        return carry

    lax.fori_loop(0, 64 // wide, hidden, 0, unroll=2)
    mine[...] = held[pl.ds(0, 2)]

    def add(t, got):
        acc[slots[t]] += got

    accumulate(tiles.shape[0], lambda t: dot_nt(held[cols[t]], tiles[t]), add)
    for s in range(16):
        agg[s] = acc[s].astype(BF16)
        got = dot(neigh[pl.ds(0, PAD), :], agg[s]).astype(BF16)
        if s < 8:
            keep[s] = got
        else:
            send[s - 8] = got


def join_second_kernel(keep, got, *out):
    for s in range(8):
        out[s // 2][s % 2] = (keep[s].astype(F32) + got[s].astype(F32)).astype(BF16)


def loss_kernel(
    classes, scale, s0, s1, s2, s3, hid, self_t, bias, labels, mask, inv, lg, w, grad, grad_bias
):
    rows = lax.broadcasted_iota(jnp.int32, (PAD, EDGE), 0)
    ones = jnp.ones((8, EDGE), BF16)
    for b in range(2):
        total = (s0[b].astype(F32) + s1[b].astype(F32)) + (s2[b].astype(F32) + s3[b].astype(F32))
        factor = inv[b : b + 1]
        logits = dot(self_t[pl.ds(0, PAD), :], hid[b]) + factor * total + bias[...]
        logits = jnp.where(rows < classes, logits, -1e30)
        e = jnp.exp(logits - jnp.max(logits, axis=0, keepdims=True))
        p = e / jnp.sum(e, axis=0, keepdims=True)
        p = p - jnp.where(rows == labels[b : b + 1], 1.0, 0.0)
        got = (p * (mask[b : b + 1].astype(F32) * scale)).astype(BF16)
        lg[b] = got
        w[b] = (got.astype(F32) * factor).astype(BF16)
        if b == 0:
            grad[...] = dot_nt(got, hid[b])
            grad_bias[...] = dot_nt(ones, got)
        else:
            grad[...] += dot_nt(got, hid[b])
            grad_bias[...] += dot_nt(ones, got)


X_ORDER = (0, 3, 1, 2)


def last_kernel(
    n_parts, slots, cols, w0, w1, w2, w3, v0, v1, v2, v3, weights, bias, tiles, agg_second, lg, self_t, neigh_t,
    grad_self, grad_bias, *refs
):
    feat_parts, agg_parts = refs[:n_parts], refs[n_parts : 2 * n_parts]
    out, both, acc, proj, both_sem = refs[2 * n_parts :]
    copies = start_pairs(feat_parts, agg_parts, both, both_sem)
    acc[...] = jnp.zeros_like(acc)
    weights_t = flip(weights[...]).astype(BF16)
    lacking = jnp.zeros((256 - PAD, EDGE), BF16)
    self_second = flip(self_t[...]).astype(BF16)
    neigh_second = flip(neigh_t[...]).astype(BF16)
    for b in range(2):
        acc[b] = dot(self_second, jnp.concatenate([lg[b], lacking], axis=0))
    g_neigh = jnp.zeros((PAD, 256), F32)
    for dx, *pair in zip(X_ORDER, (w0, w1, w2, w3), (v0, v1, v2, v3)):
        at = [(i // 2 * 4 + dx) * 2 + i % 2 for i in range(4)]
        w = jnp.concatenate([p[b] for p in pair for b in range(2)], axis=1)
        tall = jnp.concatenate([w, jnp.concatenate([lacking] * 4, axis=1)], axis=0)
        got = dot(neigh_second, tall).astype(BF16)
        for i in range(4):
            proj[at[i]] = got[:, i * EDGE : (i + 1) * EDGE]
        g_neigh += dot_nt(w, jnp.concatenate([agg_second[s] for s in at], axis=1))
    for i in range(2):
        lanes = slice(i * EDGE, (i + 1) * EDGE)
        out[pl.ds(512 + i * PAD, PAD), :] = grad_self[:, lanes].astype(BF16)
        out[pl.ds(512 + (2 + i) * PAD, PAD), :] = g_neigh[:, lanes].astype(BF16)

    def add(t, got):
        acc[cols[t]] += got

    accumulate(tiles.shape[0], lambda t: dot(proj[slots[t]], tiles[t]), add)
    for c in copies:
        c.wait()
    wide = 8
    ones = jnp.ones((8, wide * EDGE), BF16)
    bias_t = jnp.broadcast_to(bias[...], (wide * EDGE, bias.shape[1])).T

    def contract(i, carry):
        g_first, g_bias = carry
        x = both[pl.ds(i * wide, wide)].reshape(wide * EDGE, 2 * EDGE)
        back = jnp.concatenate([acc[i * wide + q] for q in range(wide)], axis=1)
        p = jnp.where(pre_first(weights_t, bias_t, x) > 0.0, back, 0.0).astype(BF16)
        return g_first + dot(p, x), g_bias + dot_nt(ones, p)

    zeros = (jnp.zeros((256, 256), F32), jnp.zeros((8, 256), F32))
    g_first, g_bias = lax.fori_loop(0, 64 // wide, contract, zeros)
    out[pl.ds(0, 256), :] = g_first[:, :EDGE].astype(BF16)
    out[pl.ds(256, 256), :] = g_first[:, EDGE:].astype(BF16)
    pick = lax.broadcasted_iota(jnp.int32, (16, EDGE), 0)
    second = jnp.concatenate([grad_bias[:1], jnp.zeros((1, 256 - PAD), F32)], axis=1)
    rows = (g_bias[:1, :EDGE], g_bias[:1, EDGE:], second[:, :EDGE], second[:, EDGE:])
    last = jnp.zeros((16, EDGE), F32)
    for i, row in enumerate(rows):
        last = jnp.where(pick == i, row, last)
    end = 512 + 4 * PAD
    out[pl.ds(end, 16), :] = last.astype(BF16)
    out[pl.ds(end + 16, 1280 - 16 - end), :] = jnp.zeros((1280 - 16 - end, EDGE), BF16)


def add_pieces_kernel(x, out):
    total = x[0].astype(F32)
    for i in range(1, x.shape[0]):
        total = total + x[i].astype(F32)
    out[...] = total.astype(BF16)


def add_arrays_kernel(a, b, c, d, out):
    total = (a[...].astype(F32) + b[...].astype(F32)) + (c[...].astype(F32) + d[...].astype(F32))
    out[...] = total.astype(BF16)


def spread_kernel(a, b, c, d, out):
    total = (a[...].astype(F32) + b[...].astype(F32)) + (c[...].astype(F32) + d[...].astype(F32))
    for i in range(out.shape[0]):
        out[i] = total.astype(BF16)


def unpack_kernel(classes, x, self_first, neigh_first, bias_first, self_t, neigh_t, bias_second):
    self_first[...] = flip(x[pl.ds(0, 256), :])
    neigh_first[...] = flip(x[pl.ds(256, 256), :])
    for at, out in ((512, self_t), (512 + 2 * PAD, neigh_t)):
        for i in range(2):
            got = x[pl.ds(at + i * PAD, PAD), :].astype(F32)
            out[:, i * EDGE : (i + 1) * EDGE] = got[:classes]
    last = x[pl.ds(512 + 4 * PAD, 16), :].astype(F32)
    bias_first[...] = jnp.concatenate([last[0:1], last[1:2]], axis=1)
    bias_second[...] = jnp.concatenate([last[2:3], last[3:4]], axis=1)


def sum_everywhere(x):
    every = ("row", "col")
    number = lambda y, z, x, c: ((y * NZ + z) * 4 + x) * 2 + c
    groups = [
        [number(y, z, x, c) for y in range(NY) for x in range(4)] for z in range(NZ) for c in range(2)
    ]
    x = x.reshape(16, -1, EDGE)
    piece = jax.ShapeDtypeStruct(x.shape[1:], BF16)
    x = lax.all_to_all(x, every, 0, 0, tiled=True, axis_index_groups=groups)
    x = call(add_pieces_kernel, piece, [VMEM])(x)
    near = [lax.ppermute(x, every, [(i, i ^ flip_bits) for i in range(256)]) for flip_bits in (1, 8, 9)]
    x = call(add_arrays_kernel, piece, [VMEM] * 4)(x, *near)
    far = [lax.ppermute(x, "row", [(i, i ^ flip_bits) for i in range(32)]) for flip_bits in (2, 6, 4)]
    x = call(spread_kernel, jax.ShapeDtypeStruct((16, 80, EDGE), BF16), [VMEM] * 4)(x, *far)
    x = lax.all_to_all(x, every, 0, 0, tiled=True, axis_index_groups=groups)
    return x.reshape(-1, EDGE)


def on_device(
    features,
    tiles,
    block_rows,
    block_cols,
    labels,
    train_mask,
    self_first,
    neigh_first,
    bias_first,
    self_second,
    neigh_second,
    bias_second,
):
    classes = self_second.shape[1]
    hid_size = self_first.shape[1]
    scale = 1.0 / math.sqrt(65536)
    row, col = lax.axis_index("row"), lax.axis_index("col")
    tiles = tiles.reshape(-1, EDGE, EDGE)
    slots = slot_of(block_rows.reshape(-1), col)
    sources = block_cols.reshape(-1)
    cols = place_of(sources, row) * 2 + sources % 2
    offs = slots // 2 * 264 + slots % 2 * EDGE
    shape = jax.ShapeDtypeStruct
    dma = pltpu.SemaphoreType.DMA
    feat = features.reshape(2, EDGE, EDGE)
    n_groups = tiles.shape[0] // GROUP

    feat_parts = ring(jnp.concatenate(along_y(feat), axis=0), ALONG_Z)
    n_feat = len(feat_parts)
    degs = [
        call(
            functools.partial(degree_kernel, i * GROUP),
            shape((16, 8, EDGE), F32),
            [SMEM, VMEM],
            mib=4,
            flops=2**32,
            bytes_accessed=2**20,
        )(slots, tiles)
        for i in range(n_groups)
    ]
    block = shape((1056, EDGE), F32)
    keep, send = call(
        functools.partial(first_kernel, n_feat),
        (block, block),
        [SMEM] * 2 + [VMEM] * 5 + [ANY] * n_feat,
        [
            pltpu.VMEM((64, EDGE, EDGE), BF16),
            pltpu.VMEM((2112, EDGE), F32),
            dma((n_feat,)),
        ],
        mib=8,
        flops=2**29,
        bytes_accessed=2**23,
    )(offs, cols, tiles, *degs, *feat_parts)
    sums = call(join_first_kernel, (shape((264, EDGE), F32),) * 4, [VMEM] * 2)(
        keep, to_sibling(send)
    )
    agg, inv = call(
        aggregate_kernel, (shape((2, EDGE, EDGE), BF16), shape((2, EDGE), F32)), [VMEM] * 4
    )(sums[0], along_x(sums[1], 1), along_x(sums[2], 2), along_x(sums[3], 3))
    agg_parts = ring(jnp.concatenate(along_y(agg), axis=0), ALONG_Z)
    weights = jnp.concatenate([self_first, neigh_first], axis=0)
    bias = bias_first.reshape(1, -1)

    lacking = ((0, 256 - classes), (0, 0))
    self_t = jnp.pad(self_second.T, lacking)
    neigh_t = jnp.pad(neigh_second.T, lacking)
    bias_wide = jnp.broadcast_to(jnp.pad(bias_second, (0, PAD - classes))[:, None], (PAD, EDGE))
    half = shape((8, PAD, EDGE), BF16)
    agg_second, keep, send, hid = call(
        functools.partial(second_kernel, n_feat),
        (shape((16, hid_size, EDGE), BF16), half, half, shape((2, hid_size, EDGE), BF16)),
        [SMEM] * 2 + [VMEM] * 4 + [ANY] * (2 * n_feat),
        [
            pltpu.VMEM((64, EDGE, 2 * EDGE), BF16),
            pltpu.VMEM((64, hid_size, EDGE), BF16),
            pltpu.VMEM((16, hid_size, EDGE), F32),
            dma((2 * n_feat,)),
        ],
        mib=18,
        flops=2**31,
        bytes_accessed=2**23,
    )(slots, cols, tiles, neigh_t, weights, bias, *feat_parts, *agg_parts)
    sums = call(join_second_kernel, (shape((2, PAD, EDGE), BF16),) * 4, [VMEM] * 2)(
        keep, to_sibling(send)
    )
    lg, w, grad_self, grad_bias = call(
        functools.partial(loss_kernel, classes, scale),
        (
            shape((2, PAD, EDGE), BF16),
            shape((2, PAD, EDGE), BF16),
            shape((PAD, hid_size), F32),
            shape((8, PAD), F32),
        ),
        [VMEM] * 10,
    )(
        sums[0],
        along_x(sums[1], 1),
        along_x(sums[2], 2),
        along_x(sums[3], 3),
        hid,
        self_t,
        bias_wide,
        labels.reshape(2, EDGE),
        train_mask.reshape(2, EDGE),
        inv,
    )
    w_parts = [w, along_x(w, 1), along_x(w, 3), along_x(w, 2)]
    w_parts += [to_sibling(p) for p in w_parts]
    grads = call(
        functools.partial(last_kernel, n_feat),
        shape((1280, EDGE), BF16),
        [SMEM] * 2 + [VMEM] * 17 + [ANY] * (2 * n_feat),
        [
            pltpu.VMEM((64, EDGE, 2 * EDGE), BF16),
            pltpu.VMEM((64, hid_size, EDGE), F32),
            pltpu.VMEM((16, hid_size, EDGE), BF16),
            dma((2 * n_feat,)),
        ],
        mib=22,
        flops=2**31,
        bytes_accessed=2**24,
    )(
        slots, cols, *w_parts, weights, bias, tiles, agg_second, lg, self_t, neigh_t, grad_self,
        grad_bias, *feat_parts, *agg_parts
    )
    out = call(
        functools.partial(unpack_kernel, classes),
        (
            shape(self_first.shape, F32),
            shape(neigh_first.shape, F32),
            shape((1, hid_size), F32),
            shape((classes, hid_size), F32),
            shape((classes, hid_size), F32),
            shape((1, 256), F32),
        ),
        [VMEM],
    )(sum_everywhere(grads))
    return (
        out[0],
        out[1],
        out[2].reshape(hid_size),
        out[3].T,
        out[4].T,
        out[5].reshape(256)[:classes],
    )


def solution(mesh):
    in_specs = (
        P(("row", "col"), None),
        P("row", "col", None, None, None),
        P("row", "col", None),
        P("row", "col", None),
        P(("row", "col")),
        P(("row", "col")),
        P(),
        P(),
        P(),
        P(),
        P(),
        P(),
    )
    out_specs = (P(), P(), P(), P(), P(), P())
    return jax.shard_map(
        on_device, mesh=mesh, in_specs=in_specs, out_specs=out_specs, check_vma=False
    )
```

```python
import functools
import math

import jax
import jax.numpy as jnp
from jax import lax
from jax.experimental import pallas as pl
from jax.experimental.pallas import tpu as pltpu
from jax.sharding import PartitionSpec as P

EDGE = 128
GROUP = 32
PAD = 176
NY, NZ = 4, 8
F32, BF16 = jnp.float32, jnp.bfloat16
VMEM = pl.BlockSpec(memory_space=pltpu.VMEM)
SMEM = pl.BlockSpec(memory_space=pltpu.SMEM)
ANY = pl.BlockSpec(memory_space=pl.ANY)
NT = (((1,), (1,)), ((), ()))


def dot(a, b):
    return jnp.dot(a, b, preferred_element_type=F32)


def dot_nt(a, b):
    return lax.dot_general(a, b, NT, preferred_element_type=F32)


def call(body, out, specs, scratch=(), mib=4, flops=0, bytes_accessed=0):
    return pl.pallas_call(
        body,
        out_shape=out,
        in_specs=specs,
        out_specs=jax.tree.map(lambda _: VMEM, out),
        scratch_shapes=list(scratch),
        compiler_params=pltpu.CompilerParams(vmem_limit_bytes=mib * 1024 * 1024),
        cost_estimate=pl.CostEstimate(
            flops=flops, bytes_accessed=bytes_accessed, transcendentals=0
        ),
    )


def step(x, groups, shift):
    pairs = [(g[i], g[(i + shift) % len(g)]) for g in groups for i in range(len(g))]
    return lax.ppermute(x, "row", pairs)


ALONG_Z = [[NZ * y + z for z in range(NZ)] for y in range(NY)]
ALONG_Y = [[NZ * y + z for y in range(NY)] for z in range(NZ)]


def ring(x, groups):
    count = len(groups[0])
    up = down = x
    parts = [x]
    for _ in range(count // 2 - 1):
        up, down = step(up, groups, 1), step(down, groups, -1)
        parts += [up, down]
    half = x.shape[0] // 2
    return parts + [step(up[:half], groups, 1), step(down[half:], groups, -1)]


def along_y(x):
    return [x, step(x, ALONG_Y, 1), step(x, ALONG_Y, -1), step(x, ALONG_Y, 2)]


def place_of(block, row):
    owner = block // 2
    dz = (owner % NZ + NZ - row % NZ) % NZ
    dy = (owner // NZ + NY - row // NZ) % NY
    z_place = jnp.where(dz <= 3, 2 * dz, jnp.where(dz == 4, 7, 15 - 2 * dz))
    y_place = jnp.where(dy == 0, 0, jnp.where(dy == 3, 1, dy + 1))
    return z_place * NY + y_place


def slot_of(block, col):
    owner = block // 2
    dx = (owner // 2 + 4 - col // 2) % 4
    dc = (owner + col) % 2
    return (dc * 4 + dx) * 2 + block % 2


def to_sibling(x):
    return lax.ppermute(x, "col", [(i, i ^ 1) for i in range(8)])


def along_x(x, shift):
    return lax.ppermute(x, "col", [(i, (i + 2 * shift) % 8) for i in range(8)])


def start_parts(parts, held, sems):
    copies, at = [], 0
    for i, p in enumerate(parts):
        n = p.shape[0]
        copies.append(pltpu.make_async_copy(p, held.at[pl.ds(at, n)], sems.at[i]))
        copies[-1].start()
        at += n
    return copies


def start_pairs(feat_parts, agg_parts, held, sems):
    copies, at = [], 0
    for i, pair in enumerate(zip(feat_parts, agg_parts)):
        n = pair[0].shape[0]
        for j, p in enumerate(pair):
            to = held.at[pl.ds(at, n), :, pl.ds(j * EDGE, EDGE)]
            copies.append(pltpu.make_async_copy(p, to, sems.at[2 * i + j]))
            copies[-1].start()
        at += n
    return copies


def accumulate(count, product, add, group=GROUP):
    def body(i, carry):
        got = [product(i * group + u) for u in range(group)]
        for u in range(group):
            add(i * group + u, got[u])
        return carry

    lax.fori_loop(0, count // group, body, 0)


def degree_kernel(first, slots, tiles, out):
    out[...] = jnp.zeros_like(out)
    ones = jnp.ones((8, EDGE), BF16)

    def product(t):
        x = tiles[first + t].astype(F32)
        x = x * x
        hi = x.astype(BF16)
        lo = (x - hi.astype(F32)).astype(BF16)
        return dot_nt(ones, hi) + dot_nt(ones, lo)

    def add(t, got):
        out[slots[first + t]] += got

    accumulate(GROUP, product, add, 8)


def first_kernel(n_parts, offs, cols, tiles, d0, d1, d2, d3, *refs):
    parts, keep, send, held, acc, sem = refs[:n_parts], *refs[n_parts:]
    copies = start_parts(parts, held, sem)
    acc[...] = jnp.zeros_like(acc)
    for s in range(16):
        deg = (d0[s][:1] + d1[s][:1]) + (d2[s][:1] + d3[s][:1])
        acc[pl.ds(s // 2 * 264 + 256 + s % 2, 1), :] = deg
    for c in copies:
        c.wait()

    def add(t, got):
        acc[pl.ds(pl.multiple_of(offs[t], 8), EDGE), :] += got

    accumulate(tiles.shape[0], lambda t: dot(tiles[t], held[cols[t]]), add)
    keep[...] = acc[pl.ds(0, 1056), :]
    send[...] = acc[pl.ds(1056, 1056), :]


def join_first_kernel(keep, got, *out):
    for x in range(4):
        at = pl.ds(x * 264, 264)
        out[x][...] = keep[at, :] + got[at, :]


def flip(x):
    return x.astype(F32).T


def flip(x):
    return x.astype(F32).T


def aggregate_kernel(s0, s1, s2, s3, agg, inv):
    total = (s0[...] + s1[...]) + (s2[...] + s3[...])
    for b in range(2):
        x = 1.0 + total[256 + b : 257 + b]
        r = lax.rsqrt(x)
        r = r * (1.5 - 0.5 * x * r * r)
        inv[pl.ds(b, 1), :] = r
        column = jnp.broadcast_to(r, (EDGE, EDGE)).T
        agg[b] = (column * total[b * EDGE : (b + 1) * EDGE]).astype(BF16)


def second_kernel(n_parts, slots, cols, tiles, neigh, weights, bias, *refs):
    feat_parts, agg_parts = refs[:n_parts], refs[n_parts : 2 * n_parts]
    agg, keep, send, mine, held, acc = refs[2 * n_parts :]
    acc[...] = jnp.zeros_like(acc)
    weights_t = flip(weights[...]).astype(BF16)
    wide = 4
    bias_t = jnp.broadcast_to(bias[...], (wide * EDGE, bias.shape[1])).T
    first = 0
    for feat_part, agg_part in zip(feat_parts, agg_parts):

        def hidden(i, carry, feat_part=feat_part, agg_part=agg_part, first=first):
            these = pl.ds(i * wide, wide)
            x = jnp.concatenate([feat_part[these], agg_part[these]], axis=2)
            x = dot_nt(weights_t, x.reshape(wide * EDGE, 2 * EDGE)) + bias_t
            h = jnp.maximum(x, 0.0).astype(BF16)
            for q in range(wide):
                held[first + i * wide + q] = h[:, q * EDGE : (q + 1) * EDGE]
            return carry

        count = feat_part.shape[0]
        lax.fori_loop(0, count // wide, hidden, 0, unroll=True)
        first += count
    mine[...] = held[pl.ds(0, 2)]

    def add(t, got):
        acc[slots[t]] += got

    accumulate(tiles.shape[0], lambda t: dot_nt(held[cols[t]], tiles[t]), add)

    def finish(s, carry):
        for out, at in ((keep, s), (send, s + 8)):
            agg[at] = acc[at].astype(BF16)
            out[s] = dot(neigh[pl.ds(0, PAD), :], agg[at]).astype(BF16)
        return carry

    lax.fori_loop(0, 8, finish, 0, unroll=2)


def join_second_kernel(keep, got, *out):
    for s in range(8):
        out[s // 2][s % 2] = (keep[s].astype(F32) + got[s].astype(F32)).astype(BF16)


def loss_kernel(
    classes, scale, s0, s1, s2, s3, hid, self_t, bias, labels, mask, inv, lg, w, grad, grad_bias
):
    rows = lax.broadcasted_iota(jnp.int32, (PAD, EDGE), 0)
    ones = jnp.ones((8, EDGE), BF16)
    for b in range(2):
        total = (s0[b].astype(F32) + s1[b].astype(F32)) + (s2[b].astype(F32) + s3[b].astype(F32))
        factor = inv[b : b + 1]
        logits = dot(self_t[pl.ds(0, PAD), :], hid[b]) + factor * total + bias[...]
        logits = jnp.where(rows < classes, logits, -1e30)
        e = jnp.exp(logits - jnp.max(logits, axis=0, keepdims=True))
        p = e / jnp.sum(e, axis=0, keepdims=True)
        p = p - jnp.where(rows == labels[b : b + 1], 1.0, 0.0)
        got = (p * (mask[b : b + 1].astype(F32) * scale)).astype(BF16)
        lg[b] = got
        w[b] = (got.astype(F32) * factor).astype(BF16)
        if b == 0:
            grad[...] = dot_nt(got, hid[b])
            grad_bias[...] = dot_nt(ones, got)
        else:
            grad[...] += dot_nt(got, hid[b])
            grad_bias[...] += dot_nt(ones, got)


X_ORDER = (0, 3, 1, 2)


def last_kernel(
    n_parts, slots, cols, w0, w1, w2, w3, v0, v1, v2, v3, held, tiles, agg_second, lg, self_t, neigh_t,
    grad_self, grad_bias, *refs
):
    feat_parts, agg_parts = refs[:n_parts], refs[n_parts : 2 * n_parts]
    out, both, acc, proj, both_sem = refs[2 * n_parts :]
    copies = start_pairs(feat_parts, agg_parts, both, both_sem)
    acc[...] = jnp.zeros_like(acc)
    lacking = jnp.zeros((256 - PAD, EDGE), BF16)
    self_second = flip(self_t[...]).astype(BF16)
    neigh_second = flip(neigh_t[...]).astype(BF16)
    for b in range(2):
        acc[b] = dot(self_second, jnp.concatenate([lg[b], lacking], axis=0))
    g_neigh = jnp.zeros((PAD, 256), F32)
    for dx, *pair in zip(X_ORDER, (w0, w1, w2, w3), (v0, v1, v2, v3)):
        at = [(i // 2 * 4 + dx) * 2 + i % 2 for i in range(4)]
        w = jnp.concatenate([p[b] for p in pair for b in range(2)], axis=1)
        tall = jnp.concatenate([w, jnp.concatenate([lacking] * 4, axis=1)], axis=0)
        got = dot(neigh_second, tall).astype(BF16)
        for i in range(4):
            proj[at[i]] = got[:, i * EDGE : (i + 1) * EDGE]
        g_neigh += dot_nt(w, jnp.concatenate([agg_second[s] for s in at], axis=1))
    for i in range(2):
        lanes = slice(i * EDGE, (i + 1) * EDGE)
        out[pl.ds(512 + i * PAD, PAD), :] = grad_self[:, lanes].astype(BF16)
        out[pl.ds(512 + (2 + i) * PAD, PAD), :] = g_neigh[:, lanes].astype(BF16)

    def add(t, got):
        acc[cols[t]] += got

    accumulate(tiles.shape[0], lambda t: dot(proj[slots[t]], tiles[t]), add)
    for c in copies:
        c.wait()
    wide = 8
    ones = jnp.ones((8, wide * EDGE), BF16)

    def contract(i, carry):
        g_first, g_bias = carry
        x = both[pl.ds(i * wide, wide)].reshape(wide * EDGE, 2 * EDGE)
        p = []
        for q in range(wide):
            s = i * wide + q
            p.append(jnp.where(held[s] > 0, acc[s].astype(BF16), jnp.zeros((), BF16)))
        p = jnp.concatenate(p, axis=1)
        return g_first + dot(p, x), g_bias + dot_nt(ones, p)

    zeros = (jnp.zeros((256, 256), F32), jnp.zeros((8, 256), F32))
    g_first, g_bias = lax.fori_loop(0, 64 // wide, contract, zeros)
    out[pl.ds(0, 256), :] = g_first[:, :EDGE].astype(BF16)
    out[pl.ds(256, 256), :] = g_first[:, EDGE:].astype(BF16)
    pick = lax.broadcasted_iota(jnp.int32, (16, EDGE), 0)
    second = jnp.concatenate([grad_bias[:1], jnp.zeros((1, 256 - PAD), F32)], axis=1)
    rows = (g_bias[:1, :EDGE], g_bias[:1, EDGE:], second[:, :EDGE], second[:, EDGE:])
    last = jnp.zeros((16, EDGE), F32)
    for i, row in enumerate(rows):
        last = jnp.where(pick == i, row, last)
    end = 512 + 4 * PAD
    out[pl.ds(end, 16), :] = last.astype(BF16)
    out[pl.ds(end + 16, 1280 - 16 - end), :] = jnp.zeros((1280 - 16 - end, EDGE), BF16)


def add_pieces_kernel(x, out):
    total = x[0].astype(F32)
    for i in range(1, x.shape[0]):
        total = total + x[i].astype(F32)
    out[...] = total.astype(BF16)


def add_arrays_kernel(a, b, c, d, out):
    total = (a[...].astype(F32) + b[...].astype(F32)) + (c[...].astype(F32) + d[...].astype(F32))
    out[...] = total.astype(BF16)


def spread_kernel(a, b, c, d, out):
    total = (a[...].astype(F32) + b[...].astype(F32)) + (c[...].astype(F32) + d[...].astype(F32))
    for i in range(out.shape[0]):
        out[i] = total.astype(BF16)


def unpack_kernel(classes, x, self_first, neigh_first, bias_first, self_t, neigh_t, bias_second):
    self_first[...] = flip(x[pl.ds(0, 256), :])
    neigh_first[...] = flip(x[pl.ds(256, 256), :])
    for at, out in ((512, self_t), (512 + 2 * PAD, neigh_t)):
        for i in range(2):
            got = x[pl.ds(at + i * PAD, PAD), :].astype(F32)
            out[:, i * EDGE : (i + 1) * EDGE] = got[:classes]
    last = x[pl.ds(512 + 4 * PAD, 16), :].astype(F32)
    bias_first[...] = jnp.concatenate([last[0:1], last[1:2]], axis=1)
    bias_second[...] = jnp.concatenate([last[2:3], last[3:4]], axis=1)


def sum_everywhere(x):
    every = ("row", "col")
    number = lambda y, z, x, c: ((y * NZ + z) * 4 + x) * 2 + c
    groups = [
        [number(y, z, x, c) for y in range(NY) for x in range(4)] for z in range(NZ) for c in range(2)
    ]
    x = x.reshape(16, -1, EDGE)
    piece = jax.ShapeDtypeStruct(x.shape[1:], BF16)
    x = lax.all_to_all(x, every, 0, 0, tiled=True, axis_index_groups=groups)
    x = call(add_pieces_kernel, piece, [VMEM])(x)
    near = [lax.ppermute(x, every, [(i, i ^ flip_bits) for i in range(256)]) for flip_bits in (1, 8, 9)]
    x = call(add_arrays_kernel, piece, [VMEM] * 4)(x, *near)
    far = [lax.ppermute(x, "row", [(i, i ^ flip_bits) for i in range(32)]) for flip_bits in (2, 6, 4)]
    x = call(spread_kernel, jax.ShapeDtypeStruct((16, 80, EDGE), BF16), [VMEM] * 4)(x, *far)
    x = lax.all_to_all(x, every, 0, 0, tiled=True, axis_index_groups=groups)
    return x.reshape(-1, EDGE)


def on_device(
    features,
    tiles,
    block_rows,
    block_cols,
    labels,
    train_mask,
    self_first,
    neigh_first,
    bias_first,
    self_second,
    neigh_second,
    bias_second,
):
    classes = self_second.shape[1]
    hid_size = self_first.shape[1]
    scale = 1.0 / math.sqrt(65536)
    row, col = lax.axis_index("row"), lax.axis_index("col")
    tiles = tiles.reshape(-1, EDGE, EDGE)
    slots = slot_of(block_rows.reshape(-1), col)
    sources = block_cols.reshape(-1)
    cols = place_of(sources, row) * 2 + sources % 2
    offs = slots // 2 * 264 + slots % 2 * EDGE
    shape = jax.ShapeDtypeStruct
    dma = pltpu.SemaphoreType.DMA
    feat = features.reshape(2, EDGE, EDGE)
    n_groups = tiles.shape[0] // GROUP

    feat_parts = ring(jnp.concatenate(along_y(feat), axis=0), ALONG_Z)
    n_feat = len(feat_parts)
    degs = [
        call(
            functools.partial(degree_kernel, i * GROUP),
            shape((16, 8, EDGE), F32),
            [SMEM, VMEM],
            mib=4,
            flops=2**32,
            bytes_accessed=2**20,
        )(slots, tiles)
        for i in range(n_groups)
    ]
    block = shape((1056, EDGE), F32)
    keep, send = call(
        functools.partial(first_kernel, n_feat),
        (block, block),
        [SMEM] * 2 + [VMEM] * 5 + [ANY] * n_feat,
        [
            pltpu.VMEM((64, EDGE, EDGE), BF16),
            pltpu.VMEM((2112, EDGE), F32),
            dma((n_feat,)),
        ],
        mib=8,
        flops=2**29,
        bytes_accessed=2**23,
    )(offs, cols, tiles, *degs, *feat_parts)
    sums = call(join_first_kernel, (shape((264, EDGE), F32),) * 4, [VMEM] * 2)(
        keep, to_sibling(send)
    )
    agg, inv = call(
        aggregate_kernel, (shape((2, EDGE, EDGE), BF16), shape((2, EDGE), F32)), [VMEM] * 4
    )(sums[0], along_x(sums[1], 1), along_x(sums[2], 2), along_x(sums[3], 3))
    agg_parts = ring(jnp.concatenate(along_y(agg), axis=0), ALONG_Z)
    weights = jnp.concatenate([self_first, neigh_first], axis=0)
    bias = bias_first.reshape(1, -1)

    lacking = ((0, 256 - classes), (0, 0))
    self_t = jnp.pad(self_second.T, lacking)
    neigh_t = jnp.pad(neigh_second.T, lacking)
    bias_wide = jnp.broadcast_to(jnp.pad(bias_second, (0, PAD - classes))[:, None], (PAD, EDGE))
    half = shape((8, PAD, EDGE), BF16)
    agg_second, keep, send, mine, hid = call(
        functools.partial(second_kernel, n_feat),
        (
            shape((16, hid_size, EDGE), BF16),
            half,
            half,
            shape((2, hid_size, EDGE), BF16),
            shape((64, hid_size, EDGE), BF16),
        ),
        [SMEM] * 2 + [VMEM] * (4 + 2 * n_feat),
        [pltpu.VMEM((16, hid_size, EDGE), F32)],
        mib=14,
        flops=2**31,
        bytes_accessed=2**23,
    )(slots, cols, tiles, neigh_t, weights, bias, *feat_parts, *agg_parts)
    sums = call(join_second_kernel, (shape((2, PAD, EDGE), BF16),) * 4, [VMEM] * 2)(
        keep, to_sibling(send)
    )
    lg, w, grad_self, grad_bias = call(
        functools.partial(loss_kernel, classes, scale),
        (
            shape((2, PAD, EDGE), BF16),
            shape((2, PAD, EDGE), BF16),
            shape((PAD, hid_size), F32),
            shape((8, PAD), F32),
        ),
        [VMEM] * 10,
    )(
        sums[0],
        along_x(sums[1], 1),
        along_x(sums[2], 2),
        along_x(sums[3], 3),
        mine,
        self_t,
        bias_wide,
        labels.reshape(2, EDGE),
        train_mask.reshape(2, EDGE),
        inv,
    )
    w_parts = [w, along_x(w, 1), along_x(w, 3), along_x(w, 2)]
    w_parts += [to_sibling(p) for p in w_parts]
    grads = call(
        functools.partial(last_kernel, n_feat),
        shape((1280, EDGE), BF16),
        [SMEM] * 2 + [VMEM] * 16 + [ANY] * (2 * n_feat),
        [
            pltpu.VMEM((64, EDGE, 2 * EDGE), BF16),
            pltpu.VMEM((64, hid_size, EDGE), F32),
            pltpu.VMEM((16, hid_size, EDGE), BF16),
            dma((2 * n_feat,)),
        ],
        mib=22,
        flops=2**31,
        bytes_accessed=2**24,
    )(
        slots, cols, *w_parts, hid, tiles, agg_second, lg, self_t, neigh_t, grad_self,
        grad_bias, *feat_parts, *agg_parts
    )
    out = call(
        functools.partial(unpack_kernel, classes),
        (
            shape(self_first.shape, F32),
            shape(neigh_first.shape, F32),
            shape((1, hid_size), F32),
            shape((classes, hid_size), F32),
            shape((classes, hid_size), F32),
            shape((1, 256), F32),
        ),
        [VMEM],
    )(sum_everywhere(grads))
    return (
        out[0],
        out[1],
        out[2].reshape(hid_size),
        out[3].T,
        out[4].T,
        out[5].reshape(256)[:classes],
    )


def solution(mesh):
    in_specs = (
        P(("row", "col"), None),
        P("row", "col", None, None, None),
        P("row", "col", None),
        P("row", "col", None),
        P(("row", "col")),
        P(("row", "col")),
        P(),
        P(),
        P(),
        P(),
        P(),
        P(),
    )
    out_specs = (P(), P(), P(), P(), P(), P())
    return jax.shard_map(
        on_device, mesh=mesh, in_specs=in_specs, out_specs=out_specs, check_vma=False
    )
```

```python
import functools
import math

import jax
import jax.numpy as jnp
from jax import lax
from jax.experimental import pallas as pl
from jax.experimental.pallas import tpu as pltpu
from jax.sharding import PartitionSpec as P

EDGE = 128
GROUP = 32
PAD = 176
NY, NZ = 4, 8
F32, BF16 = jnp.float32, jnp.bfloat16
VMEM = pl.BlockSpec(memory_space=pltpu.VMEM)
SMEM = pl.BlockSpec(memory_space=pltpu.SMEM)
ANY = pl.BlockSpec(memory_space=pl.ANY)
NT = (((1,), (1,)), ((), ()))


def dot(a, b):
    return jnp.dot(a, b, preferred_element_type=F32)


def dot_nt(a, b):
    return lax.dot_general(a, b, NT, preferred_element_type=F32)


def call(body, out, specs, scratch=(), mib=4, flops=0, bytes_accessed=0):
    return pl.pallas_call(
        body,
        out_shape=out,
        in_specs=specs,
        out_specs=jax.tree.map(lambda _: VMEM, out),
        scratch_shapes=list(scratch),
        compiler_params=pltpu.CompilerParams(vmem_limit_bytes=mib * 1024 * 1024),
        cost_estimate=pl.CostEstimate(
            flops=flops, bytes_accessed=bytes_accessed, transcendentals=0
        ),
    )


def step(x, groups, shift):
    pairs = [(g[i], g[(i + shift) % len(g)]) for g in groups for i in range(len(g))]
    return lax.ppermute(x, "row", pairs)


ALONG_Z = [[NZ * y + z for z in range(NZ)] for y in range(NY)]
ALONG_Y = [[NZ * y + z for y in range(NY)] for z in range(NZ)]


def ring(x, groups):
    count = len(groups[0])
    up = down = x
    parts = [x]
    for _ in range(count // 2 - 1):
        up, down = step(up, groups, 1), step(down, groups, -1)
        parts += [up, down]
    half = x.shape[0] // 2
    return parts + [step(up[:half], groups, 1), step(down[half:], groups, -1)]


def along_y(x):
    return [x, step(x, ALONG_Y, 1), step(x, ALONG_Y, -1), step(x, ALONG_Y, 2)]


def place_of(block, row):
    owner = block // 2
    dz = (owner % NZ + NZ - row % NZ) % NZ
    dy = (owner // NZ + NY - row // NZ) % NY
    z_place = jnp.where(dz <= 3, 2 * dz, jnp.where(dz == 4, 7, 15 - 2 * dz))
    y_place = jnp.where(dy == 0, 0, jnp.where(dy == 3, 1, dy + 1))
    return z_place * NY + y_place


def slot_of(block, col):
    owner = block // 2
    dx = (owner // 2 + 4 - col // 2) % 4
    dc = (owner + col) % 2
    return (dc * 4 + dx) * 2 + block % 2


def to_sibling(x):
    return lax.ppermute(x, "col", [(i, i ^ 1) for i in range(8)])


def along_x(x, shift):
    return lax.ppermute(x, "col", [(i, (i + 2 * shift) % 8) for i in range(8)])


def start_parts(parts, held, sems):
    copies, at = [], 0
    for i, p in enumerate(parts):
        n = p.shape[0]
        copies.append(pltpu.make_async_copy(p, held.at[pl.ds(at, n)], sems.at[i]))
        copies[-1].start()
        at += n
    return copies


def start_pairs(feat_parts, agg_parts, held, sems):
    copies, at = [], 0
    for i, pair in enumerate(zip(feat_parts, agg_parts)):
        n = pair[0].shape[0]
        for j, p in enumerate(pair):
            to = held.at[pl.ds(at, n), :, pl.ds(j * EDGE, EDGE)]
            copies.append(pltpu.make_async_copy(p, to, sems.at[2 * i + j]))
            copies[-1].start()
        at += n
    return copies


def accumulate(count, product, add, group=GROUP):
    def body(i, carry):
        got = [product(i * group + u) for u in range(group)]
        for u in range(group):
            add(i * group + u, got[u])
        return carry

    lax.fori_loop(0, count // group, body, 0)


def degree_kernel(first, slots, tiles, out):
    out[...] = jnp.zeros_like(out)
    ones = jnp.ones((8, EDGE), BF16)

    def product(t):
        x = tiles[first + t].astype(F32)
        x = x * x
        hi = x.astype(BF16)
        lo = (x - hi.astype(F32)).astype(BF16)
        return dot_nt(ones, hi) + dot_nt(ones, lo)

    def add(t, got):
        out[slots[first + t]] += got

    accumulate(GROUP, product, add, 4)


def first_kernel(n_parts, offs, cols, tiles, d0, d1, d2, d3, *refs):
    parts, keep, send, held, acc, sem = refs[:n_parts], *refs[n_parts:]
    copies = start_parts(parts, held, sem)
    acc[...] = jnp.zeros_like(acc)
    for s in range(16):
        deg = (d0[s][:1] + d1[s][:1]) + (d2[s][:1] + d3[s][:1])
        acc[pl.ds(s // 2 * 264 + 256 + s % 2, 1), :] = deg
    for c in copies:
        c.wait()

    def add(t, got):
        acc[pl.ds(pl.multiple_of(offs[t], 8), EDGE), :] += got

    accumulate(tiles.shape[0], lambda t: dot(tiles[t], held[cols[t]]), add)
    keep[...] = acc[pl.ds(0, 1056), :]
    send[...] = acc[pl.ds(1056, 1056), :]


def join_first_kernel(keep, got, *out):
    for x in range(4):
        at = pl.ds(x * 264, 264)
        out[x][...] = keep[at, :] + got[at, :]


def flip(x):
    return x.astype(F32).T


def flip(x):
    return x.astype(F32).T


def aggregate_kernel(s0, s1, s2, s3, agg, inv):
    total = (s0[...] + s1[...]) + (s2[...] + s3[...])
    for b in range(2):
        x = 1.0 + total[256 + b : 257 + b]
        r = lax.rsqrt(x)
        r = r * (1.5 - 0.5 * x * r * r)
        inv[pl.ds(b, 1), :] = r
        column = jnp.broadcast_to(r, (EDGE, EDGE)).T
        agg[b] = (column * total[b * EDGE : (b + 1) * EDGE]).astype(BF16)


def second_kernel(n_parts, slots, cols, tiles, neigh, weights, bias, *refs):
    feat_parts, agg_parts = refs[:n_parts], refs[n_parts : 2 * n_parts]
    agg, keep, send, mine, held, acc = refs[2 * n_parts :]
    acc[...] = jnp.zeros_like(acc)
    weights_t = flip(weights[...]).astype(BF16)
    wide = 4
    bias_t = jnp.broadcast_to(bias[...], (wide * EDGE, bias.shape[1])).T
    first = 0
    for feat_part, agg_part in zip(feat_parts, agg_parts):

        def hidden(i, carry, feat_part=feat_part, agg_part=agg_part, first=first):
            these = pl.ds(i * wide, wide)
            x = jnp.concatenate([feat_part[these], agg_part[these]], axis=2)
            x = dot_nt(weights_t, x.reshape(wide * EDGE, 2 * EDGE)) + bias_t
            h = jnp.maximum(x, 0.0).astype(BF16)
            for q in range(wide):
                held[first + i * wide + q] = h[:, q * EDGE : (q + 1) * EDGE]
            return carry

        count = feat_part.shape[0]
        lax.fori_loop(0, count // wide, hidden, 0, unroll=True)
        first += count
    mine[...] = held[pl.ds(0, 2)]

    def add(t, got):
        acc[slots[t]] += got

    accumulate(tiles.shape[0], lambda t: dot_nt(held[cols[t]], tiles[t]), add)

    def finish(s, carry):
        for out, at in ((keep, s), (send, s + 8)):
            agg[at] = acc[at].astype(BF16)
            out[s] = dot(neigh[pl.ds(0, PAD), :], agg[at]).astype(BF16)
        return carry

    lax.fori_loop(0, 8, finish, 0)


def join_second_kernel(keep, got, *out):
    for s in range(8):
        out[s // 2][s % 2] = (keep[s].astype(F32) + got[s].astype(F32)).astype(BF16)


def loss_kernel(
    classes, scale, s0, s1, s2, s3, hid, self_t, bias, labels, mask, inv, lg, w, grad, grad_bias
):
    rows = lax.broadcasted_iota(jnp.int32, (PAD, EDGE), 0)
    ones = jnp.ones((8, EDGE), BF16)
    for b in range(2):
        total = (s0[b].astype(F32) + s1[b].astype(F32)) + (s2[b].astype(F32) + s3[b].astype(F32))
        factor = inv[b : b + 1]
        logits = dot(self_t[pl.ds(0, PAD), :], hid[b]) + factor * total + bias[...]
        logits = jnp.where(rows < classes, logits, -1e30)
        e = jnp.exp(logits - jnp.max(logits, axis=0, keepdims=True))
        p = e / jnp.sum(e, axis=0, keepdims=True)
        p = p - jnp.where(rows == labels[b : b + 1], 1.0, 0.0)
        got = (p * (mask[b : b + 1].astype(F32) * scale)).astype(BF16)
        lg[b] = got
        w[b] = (got.astype(F32) * factor).astype(BF16)
        if b == 0:
            grad[...] = dot_nt(got, hid[b])
            grad_bias[...] = dot_nt(ones, got)
        else:
            grad[...] += dot_nt(got, hid[b])
            grad_bias[...] += dot_nt(ones, got)


X_ORDER = (0, 3, 1, 2)


def last_kernel(
    n_parts, slots, cols, w0, w1, w2, w3, sibling, held, tiles, agg_second, lg, self_t, neigh_t,
    grad_self, grad_bias, *refs
):
    feat_parts, agg_parts = refs[:n_parts], refs[n_parts : 2 * n_parts]
    out, both, acc, proj, both_sem = refs[2 * n_parts :]
    copies = start_pairs(feat_parts, agg_parts, both, both_sem)
    acc[...] = jnp.zeros_like(acc)
    lacking = jnp.zeros((256 - PAD, EDGE), BF16)
    self_second = flip(self_t[...]).astype(BF16)
    neigh_second = flip(neigh_t[...]).astype(BF16)
    for b in range(2):
        acc[b] = dot(self_second, jnp.concatenate([lg[b], lacking], axis=0))
    g_neigh = jnp.zeros((PAD, 256), F32)
    for i, (dx, part) in enumerate(zip(X_ORDER, (w0, w1, w2, w3))):
        at = [(j // 2 * 4 + dx) * 2 + j % 2 for j in range(4)]
        w = jnp.concatenate([part[0], part[1], sibling[2 * i], sibling[2 * i + 1]], axis=1)
        tall = jnp.concatenate([w, jnp.concatenate([lacking] * 4, axis=1)], axis=0)
        got = dot(neigh_second, tall).astype(BF16)
        for j in range(4):
            proj[at[j]] = got[:, j * EDGE : (j + 1) * EDGE]
        g_neigh += dot_nt(w, jnp.concatenate([agg_second[s] for s in at], axis=1))
    for i in range(2):
        lanes = slice(i * EDGE, (i + 1) * EDGE)
        out[pl.ds(512 + i * PAD, PAD), :] = grad_self[:, lanes].astype(BF16)
        out[pl.ds(512 + (2 + i) * PAD, PAD), :] = g_neigh[:, lanes].astype(BF16)

    def add(t, got):
        acc[cols[t]] += got

    accumulate(tiles.shape[0], lambda t: dot(proj[slots[t]], tiles[t]), add)
    for c in copies:
        c.wait()
    wide = 8
    ones = jnp.ones((8, wide * EDGE), BF16)

    def contract(i, carry):
        g_first, g_bias = carry
        x = both[pl.ds(i * wide, wide)].reshape(wide * EDGE, 2 * EDGE)
        p = []
        for q in range(wide):
            s = i * wide + q
            p.append(jnp.where(held[s] > 0, acc[s].astype(BF16), jnp.zeros((), BF16)))
        p = jnp.concatenate(p, axis=1)
        return g_first + dot(p, x), g_bias + dot_nt(ones, p)

    zeros = (jnp.zeros((256, 256), F32), jnp.zeros((8, 256), F32))
    g_first, g_bias = lax.fori_loop(0, 64 // wide, contract, zeros)
    out[pl.ds(0, 256), :] = g_first[:, :EDGE].astype(BF16)
    out[pl.ds(256, 256), :] = g_first[:, EDGE:].astype(BF16)
    pick = lax.broadcasted_iota(jnp.int32, (16, EDGE), 0)
    second = jnp.concatenate([grad_bias[:1], jnp.zeros((1, 256 - PAD), F32)], axis=1)
    rows = (g_bias[:1, :EDGE], g_bias[:1, EDGE:], second[:, :EDGE], second[:, EDGE:])
    last = jnp.zeros((16, EDGE), F32)
    for i, row in enumerate(rows):
        last = jnp.where(pick == i, row, last)
    end = 512 + 4 * PAD
    out[pl.ds(end, 16), :] = last.astype(BF16)
    out[pl.ds(end + 16, 1280 - 16 - end), :] = jnp.zeros((1280 - 16 - end, EDGE), BF16)


def add_pieces_kernel(x, out):
    total = x[0].astype(F32)
    for i in range(1, x.shape[0]):
        total = total + x[i].astype(F32)
    out[...] = total.astype(BF16)


def add_arrays_kernel(a, b, c, d, out):
    total = (a[...].astype(F32) + b[...].astype(F32)) + (c[...].astype(F32) + d[...].astype(F32))
    out[...] = total.astype(BF16)


def spread_kernel(a, b, c, d, out):
    total = (a[...].astype(F32) + b[...].astype(F32)) + (c[...].astype(F32) + d[...].astype(F32))
    for i in range(out.shape[0]):
        out[i] = total.astype(BF16)


def unpack_kernel(classes, x, self_first, neigh_first, bias_first, self_t, neigh_t, bias_second):
    self_first[...] = flip(x[pl.ds(0, 256), :])
    neigh_first[...] = flip(x[pl.ds(256, 256), :])
    for at, out in ((512, self_t), (512 + 2 * PAD, neigh_t)):
        for i in range(2):
            got = x[pl.ds(at + i * PAD, PAD), :].astype(F32)
            out[:, i * EDGE : (i + 1) * EDGE] = got[:classes]
    last = x[pl.ds(512 + 4 * PAD, 16), :].astype(F32)
    bias_first[...] = jnp.concatenate([last[0:1], last[1:2]], axis=1)
    bias_second[...] = jnp.concatenate([last[2:3], last[3:4]], axis=1)


def sum_everywhere(x):
    every = ("row", "col")
    number = lambda y, z, x, c: ((y * NZ + z) * 4 + x) * 2 + c
    groups = [
        [number(y, z, x, c) for y in range(NY) for x in range(4)] for z in range(NZ) for c in range(2)
    ]
    x = x.reshape(16, -1, EDGE)
    piece = jax.ShapeDtypeStruct(x.shape[1:], BF16)
    x = lax.all_to_all(x, every, 0, 0, tiled=True, axis_index_groups=groups)
    x = call(add_pieces_kernel, piece, [VMEM])(x)
    near = [lax.ppermute(x, every, [(i, i ^ flip_bits) for i in range(256)]) for flip_bits in (1, 8, 9)]
    x = call(add_arrays_kernel, piece, [VMEM] * 4)(x, *near)
    far = [lax.ppermute(x, "row", [(i, i ^ flip_bits) for i in range(32)]) for flip_bits in (2, 6, 4)]
    x = call(spread_kernel, jax.ShapeDtypeStruct((16, 80, EDGE), BF16), [VMEM] * 4)(x, *far)
    x = lax.all_to_all(x, every, 0, 0, tiled=True, axis_index_groups=groups)
    return x.reshape(-1, EDGE)


def on_device(
    features,
    tiles,
    block_rows,
    block_cols,
    labels,
    train_mask,
    self_first,
    neigh_first,
    bias_first,
    self_second,
    neigh_second,
    bias_second,
):
    classes = self_second.shape[1]
    hid_size = self_first.shape[1]
    scale = 1.0 / math.sqrt(65536)
    row, col = lax.axis_index("row"), lax.axis_index("col")
    tiles = tiles.reshape(-1, EDGE, EDGE)
    slots = slot_of(block_rows.reshape(-1), col)
    sources = block_cols.reshape(-1)
    cols = place_of(sources, row) * 2 + sources % 2
    offs = slots // 2 * 264 + slots % 2 * EDGE
    shape = jax.ShapeDtypeStruct
    dma = pltpu.SemaphoreType.DMA
    feat = features.reshape(2, EDGE, EDGE)
    n_groups = tiles.shape[0] // GROUP

    feat_parts = ring(jnp.concatenate(along_y(feat), axis=0), ALONG_Z)
    n_feat = len(feat_parts)
    degs = [
        call(
            functools.partial(degree_kernel, i * GROUP),
            shape((16, 8, EDGE), F32),
            [SMEM, VMEM],
            mib=4,
            flops=2**32,
            bytes_accessed=2**20,
        )(slots, tiles)
        for i in range(n_groups)
    ]
    block = shape((1056, EDGE), F32)
    keep, send = call(
        functools.partial(first_kernel, n_feat),
        (block, block),
        [SMEM] * 2 + [VMEM] * 5 + [ANY] * n_feat,
        [
            pltpu.VMEM((64, EDGE, EDGE), BF16),
            pltpu.VMEM((2112, EDGE), F32),
            dma((n_feat,)),
        ],
        mib=8,
        flops=2**29,
        bytes_accessed=2**23,
    )(offs, cols, tiles, *degs, *feat_parts)
    sums = call(join_first_kernel, (shape((264, EDGE), F32),) * 4, [VMEM] * 2)(
        keep, to_sibling(send)
    )
    agg, inv = call(
        aggregate_kernel, (shape((2, EDGE, EDGE), BF16), shape((2, EDGE), F32)), [VMEM] * 4
    )(sums[0], along_x(sums[1], 1), along_x(sums[2], 2), along_x(sums[3], 3))
    agg_parts = ring(jnp.concatenate(along_y(agg), axis=0), ALONG_Z)
    weights = jnp.concatenate([self_first, neigh_first], axis=0)
    bias = bias_first.reshape(1, -1)

    lacking = ((0, 256 - classes), (0, 0))
    self_t = jnp.pad(self_second.T, lacking)
    neigh_t = jnp.pad(neigh_second.T, lacking)
    bias_wide = jnp.broadcast_to(jnp.pad(bias_second, (0, PAD - classes))[:, None], (PAD, EDGE))
    half = shape((8, PAD, EDGE), BF16)
    agg_second, keep, send, mine, hid = call(
        functools.partial(second_kernel, n_feat),
        (
            shape((16, hid_size, EDGE), BF16),
            half,
            half,
            shape((2, hid_size, EDGE), BF16),
            shape((64, hid_size, EDGE), BF16),
        ),
        [SMEM] * 2 + [VMEM] * (4 + 2 * n_feat),
        [pltpu.VMEM((16, hid_size, EDGE), F32)],
        mib=14,
        flops=2**31,
        bytes_accessed=2**23,
    )(slots, cols, tiles, neigh_t, weights, bias, *feat_parts, *agg_parts)
    sums = call(join_second_kernel, (shape((2, PAD, EDGE), BF16),) * 4, [VMEM] * 2)(
        keep, to_sibling(send)
    )
    lg, w, grad_self, grad_bias = call(
        functools.partial(loss_kernel, classes, scale),
        (
            shape((2, PAD, EDGE), BF16),
            shape((2, PAD, EDGE), BF16),
            shape((PAD, hid_size), F32),
            shape((8, PAD), F32),
        ),
        [VMEM] * 10,
    )(
        sums[0],
        along_x(sums[1], 1),
        along_x(sums[2], 2),
        along_x(sums[3], 3),
        mine,
        self_t,
        bias_wide,
        labels.reshape(2, EDGE),
        train_mask.reshape(2, EDGE),
        inv,
    )
    w_parts = [w, along_x(w, 1), along_x(w, 3), along_x(w, 2)]
    w_parts.append(to_sibling(jnp.concatenate(w_parts, axis=0)))
    grads = call(
        functools.partial(last_kernel, n_feat),
        shape((1280, EDGE), BF16),
        [SMEM] * 2 + [VMEM] * 13 + [ANY] * (2 * n_feat),
        [
            pltpu.VMEM((64, EDGE, 2 * EDGE), BF16),
            pltpu.VMEM((64, hid_size, EDGE), F32),
            pltpu.VMEM((16, hid_size, EDGE), BF16),
            dma((2 * n_feat,)),
        ],
        mib=22,
        flops=2**31,
        bytes_accessed=2**24,
    )(
        slots, cols, *w_parts, hid, tiles, agg_second, lg, self_t, neigh_t, grad_self,
        grad_bias, *feat_parts, *agg_parts
    )
    out = call(
        functools.partial(unpack_kernel, classes),
        (
            shape(self_first.shape, F32),
            shape(neigh_first.shape, F32),
            shape((1, hid_size), F32),
            shape((classes, hid_size), F32),
            shape((classes, hid_size), F32),
            shape((1, 256), F32),
        ),
        [VMEM],
    )(sum_everywhere(grads))
    return (
        out[0],
        out[1],
        out[2].reshape(hid_size),
        out[3].T,
        out[4].T,
        out[5].reshape(256)[:classes],
    )


def solution(mesh):
    in_specs = (
        P(("row", "col"), None),
        P("row", "col", None, None, None),
        P("row", "col", None),
        P("row", "col", None),
        P(("row", "col")),
        P(("row", "col")),
        P(),
        P(),
        P(),
        P(),
        P(),
        P(),
    )
    out_specs = (P(), P(), P(), P(), P(), P())
    return jax.shard_map(
        on_device, mesh=mesh, in_specs=in_specs, out_specs=out_specs, check_vma=False
    )
```

```python
import functools
import math

import jax
import jax.numpy as jnp
from jax import lax
from jax.experimental import pallas as pl
from jax.experimental.pallas import tpu as pltpu
from jax.sharding import PartitionSpec as P

EDGE = 128
GROUP = 32
PAD = 176
NY, NZ = 4, 8
F32, BF16 = jnp.float32, jnp.bfloat16
VMEM = pl.BlockSpec(memory_space=pltpu.VMEM)
SMEM = pl.BlockSpec(memory_space=pltpu.SMEM)
ANY = pl.BlockSpec(memory_space=pl.ANY)
NT = (((1,), (1,)), ((), ()))


def dot(a, b):
    return jnp.dot(a, b, preferred_element_type=F32)


def dot_nt(a, b):
    return lax.dot_general(a, b, NT, preferred_element_type=F32)


def call(body, out, specs, scratch=(), mib=4, flops=0, bytes_accessed=0):
    return pl.pallas_call(
        body,
        out_shape=out,
        in_specs=specs,
        out_specs=jax.tree.map(lambda _: VMEM, out),
        scratch_shapes=list(scratch),
        compiler_params=pltpu.CompilerParams(vmem_limit_bytes=mib * 1024 * 1024),
        cost_estimate=pl.CostEstimate(
            flops=flops, bytes_accessed=bytes_accessed, transcendentals=0
        ),
    )


def step(x, groups, shift):
    pairs = [(g[i], g[(i + shift) % len(g)]) for g in groups for i in range(len(g))]
    return lax.ppermute(x, "row", pairs)


ALONG_Z = [[NZ * y + z for z in range(NZ)] for y in range(NY)]
ALONG_Y = [[NZ * y + z for y in range(NY)] for z in range(NZ)]


def ring(x, groups):
    count = len(groups[0])
    up = down = x
    parts = [x]
    for _ in range(count // 2 - 1):
        up, down = step(up, groups, 1), step(down, groups, -1)
        parts += [up, down]
    half = x.shape[0] // 2
    return parts + [step(up[:half], groups, 1), step(down[half:], groups, -1)]


def along_y(x):
    return [x, step(x, ALONG_Y, 1), step(x, ALONG_Y, -1), step(x, ALONG_Y, 2)]


def place_of(block, row):
    owner = block // 2
    dz = (owner % NZ + NZ - row % NZ) % NZ
    dy = (owner // NZ + NY - row // NZ) % NY
    z_place = jnp.where(dz <= 3, 2 * dz, jnp.where(dz == 4, 7, 15 - 2 * dz))
    y_place = jnp.where(dy == 0, 0, jnp.where(dy == 3, 1, dy + 1))
    return z_place * NY + y_place


def slot_of(block, col):
    owner = block // 2
    dx = (owner // 2 + 4 - col // 2) % 4
    dc = (owner + col) % 2
    return (dc * 4 + dx) * 2 + block % 2


def to_sibling(x):
    return lax.ppermute(x, "col", [(i, i ^ 1) for i in range(8)])


def along_x(x, shift):
    return lax.ppermute(x, "col", [(i, (i + 2 * shift) % 8) for i in range(8)])


def start_parts(parts, held, sems):
    copies, at = [], 0
    for i, p in enumerate(parts):
        n = p.shape[0]
        copies.append(pltpu.make_async_copy(p, held.at[pl.ds(at, n)], sems.at[i]))
        copies[-1].start()
        at += n
    return copies


def start_pairs(feat_parts, agg_parts, held, sems):
    copies, at = [], 0
    for i, pair in enumerate(zip(feat_parts, agg_parts)):
        n = pair[0].shape[0]
        for j, p in enumerate(pair):
            to = held.at[pl.ds(at, n), :, pl.ds(j * EDGE, EDGE)]
            copies.append(pltpu.make_async_copy(p, to, sems.at[2 * i + j]))
            copies[-1].start()
        at += n
    return copies


def accumulate(count, product, add, group=GROUP):
    def body(i, carry):
        got = [product(i * group + u) for u in range(group)]
        for u in range(group):
            add(i * group + u, got[u])
        return carry

    lax.fori_loop(0, count // group, body, 0)


def degree_kernel(first, slots, tiles, out):
    out[...] = jnp.zeros_like(out)
    ones = jnp.ones((8, EDGE), BF16)

    def product(t):
        x = tiles[first + t].astype(F32)
        x = x * x
        hi = x.astype(BF16)
        lo = (x - hi.astype(F32)).astype(BF16)
        return dot_nt(ones, hi) + dot_nt(ones, lo)

    def add(t, got):
        out[slots[first + t]] += got

    accumulate(GROUP, product, add, 4)


def first_kernel(n_parts, offs, cols, tiles, d0, d1, d2, d3, *refs):
    parts, keep, send, held, acc, sem = refs[:n_parts], *refs[n_parts:]
    copies = start_parts(parts, held, sem)
    acc[...] = jnp.zeros_like(acc)
    for s in range(16):
        deg = (d0[s][:1] + d1[s][:1]) + (d2[s][:1] + d3[s][:1])
        acc[pl.ds(s // 2 * 264 + 256 + s % 2, 1), :] = deg
    for c in copies:
        c.wait()

    def add(t, got):
        acc[pl.ds(pl.multiple_of(offs[t], 8), EDGE), :] += got

    accumulate(tiles.shape[0], lambda t: dot(tiles[t], held[cols[t]]), add)
    keep[...] = acc[pl.ds(0, 1056), :]
    send[...] = acc[pl.ds(1056, 1056), :]


def join_first_kernel(keep, got, *out):
    for x in range(4):
        at = pl.ds(x * 264, 264)
        out[x][...] = keep[at, :] + got[at, :]


def flip(x):
    return x.astype(F32).T


def flip(x):
    return x.astype(F32).T


def weights_kernel(first, bias, self_t, neigh_t, first_t, bias_t, self_second, neigh_second):
    first_t[...] = flip(first[...]).astype(BF16)
    bias_t[...] = jnp.broadcast_to(bias[...], (EDGE, bias.shape[1])).T
    self_second[...] = flip(self_t[...]).astype(BF16)
    neigh_second[...] = flip(neigh_t[...]).astype(BF16)


def aggregate_kernel(s0, s1, s2, s3, agg, inv):
    total = (s0[...] + s1[...]) + (s2[...] + s3[...])
    for b in range(2):
        x = 1.0 + total[256 + b : 257 + b]
        r = lax.rsqrt(x)
        r = r * (1.5 - 0.5 * x * r * r)
        inv[pl.ds(b, 1), :] = r
        column = jnp.broadcast_to(r, (EDGE, EDGE)).T
        agg[b] = (column * total[b * EDGE : (b + 1) * EDGE]).astype(BF16)


def second_kernel(n_parts, slots, cols, tiles, neigh, weights, bias, *refs):
    feat_parts, agg_parts = refs[:n_parts], refs[n_parts : 2 * n_parts]
    agg, keep, send, mine, held, acc = refs[2 * n_parts :]
    acc[...] = jnp.zeros_like(acc)
    weights_t = weights[...]
    wide = 4
    bias_t = jnp.concatenate([bias[...]] * wide, axis=1)
    first = 0
    for feat_part, agg_part in zip(feat_parts, agg_parts):

        def hidden(i, carry, feat_part=feat_part, agg_part=agg_part, first=first):
            these = pl.ds(i * wide, wide)
            x = jnp.concatenate([feat_part[these], agg_part[these]], axis=2)
            x = dot_nt(weights_t, x.reshape(wide * EDGE, 2 * EDGE)) + bias_t
            h = jnp.maximum(x, 0.0).astype(BF16)
            for q in range(wide):
                held[first + i * wide + q] = h[:, q * EDGE : (q + 1) * EDGE]
            return carry

        count = feat_part.shape[0]
        lax.fori_loop(0, count // wide, hidden, 0, unroll=True)
        first += count
    mine[...] = held[pl.ds(0, 2)]

    def add(t, got):
        acc[slots[t]] += got

    accumulate(tiles.shape[0], lambda t: dot_nt(held[cols[t]], tiles[t]), add)

    def finish(s, carry):
        for out, at in ((keep, s), (send, s + 8)):
            agg[at] = acc[at].astype(BF16)
            out[s] = dot(neigh[pl.ds(0, PAD), :], agg[at]).astype(BF16)
        return carry

    lax.fori_loop(0, 8, finish, 0)


def join_second_kernel(keep, got, *out):
    for s in range(8):
        out[s // 2][s % 2] = (keep[s].astype(F32) + got[s].astype(F32)).astype(BF16)


def loss_kernel(
    classes, scale, s0, s1, s2, s3, hid, self_t, bias, labels, mask, inv, lg, w, grad, grad_bias
):
    rows = lax.broadcasted_iota(jnp.int32, (PAD, EDGE), 0)
    ones = jnp.ones((8, EDGE), BF16)
    for b in range(2):
        total = (s0[b].astype(F32) + s1[b].astype(F32)) + (s2[b].astype(F32) + s3[b].astype(F32))
        factor = inv[b : b + 1]
        logits = dot(self_t[pl.ds(0, PAD), :], hid[b]) + factor * total + bias[...]
        logits = jnp.where(rows < classes, logits, -1e30)
        e = jnp.exp(logits - jnp.max(logits, axis=0, keepdims=True))
        p = e / jnp.sum(e, axis=0, keepdims=True)
        p = p - jnp.where(rows == labels[b : b + 1], 1.0, 0.0)
        got = (p * (mask[b : b + 1].astype(F32) * scale)).astype(BF16)
        lg[b] = got
        w[b] = (got.astype(F32) * factor).astype(BF16)
        if b == 0:
            grad[...] = dot_nt(got, hid[b])
            grad_bias[...] = dot_nt(ones, got)
        else:
            grad[...] += dot_nt(got, hid[b])
            grad_bias[...] += dot_nt(ones, got)


X_ORDER = (0, 3, 1, 2)


def last_kernel(
    n_parts, slots, cols, w0, w1, w2, w3, sibling, held, tiles, agg_second, lg, self_second, neigh_second,
    grad_self, grad_bias, *refs
):
    feat_parts, agg_parts = refs[:n_parts], refs[n_parts : 2 * n_parts]
    out, both, acc, proj, both_sem = refs[2 * n_parts :]
    copies = start_pairs(feat_parts, agg_parts, both, both_sem)
    acc[...] = jnp.zeros_like(acc)
    lacking = jnp.zeros((256 - PAD, EDGE), BF16)
    for b in range(2):
        acc[b] = dot(self_second[...], jnp.concatenate([lg[b], lacking], axis=0))
    g_neigh = jnp.zeros((PAD, 256), F32)
    for i, (dx, part) in enumerate(zip(X_ORDER, (w0, w1, w2, w3))):
        at = [(j // 2 * 4 + dx) * 2 + j % 2 for j in range(4)]
        w = jnp.concatenate([part[0], part[1], sibling[2 * i], sibling[2 * i + 1]], axis=1)
        tall = jnp.concatenate([w, jnp.concatenate([lacking] * 4, axis=1)], axis=0)
        got = dot(neigh_second[...], tall).astype(BF16)
        for j in range(4):
            proj[at[j]] = got[:, j * EDGE : (j + 1) * EDGE]
        g_neigh += dot_nt(w, jnp.concatenate([agg_second[s] for s in at], axis=1))
    for i in range(2):
        lanes = slice(i * EDGE, (i + 1) * EDGE)
        out[pl.ds(512 + i * PAD, PAD), :] = grad_self[:, lanes].astype(BF16)
        out[pl.ds(512 + (2 + i) * PAD, PAD), :] = g_neigh[:, lanes].astype(BF16)

    def add(t, got):
        acc[cols[t]] += got

    accumulate(tiles.shape[0], lambda t: dot(proj[slots[t]], tiles[t]), add)
    for c in copies:
        c.wait()
    wide = 8
    ones = jnp.ones((8, wide * EDGE), BF16)

    def contract(i, carry):
        g_first, g_bias = carry
        x = both[pl.ds(i * wide, wide)].reshape(wide * EDGE, 2 * EDGE)
        p = []
        for q in range(wide):
            s = i * wide + q
            p.append(jnp.where(held[s] > 0, acc[s].astype(BF16), jnp.zeros((), BF16)))
        p = jnp.concatenate(p, axis=1)
        return g_first + dot(p, x), g_bias + dot_nt(ones, p)

    zeros = (jnp.zeros((256, 256), F32), jnp.zeros((8, 256), F32))
    g_first, g_bias = lax.fori_loop(0, 64 // wide, contract, zeros)
    out[pl.ds(0, 256), :] = g_first[:, :EDGE].astype(BF16)
    out[pl.ds(256, 256), :] = g_first[:, EDGE:].astype(BF16)
    pick = lax.broadcasted_iota(jnp.int32, (16, EDGE), 0)
    second = jnp.concatenate([grad_bias[:1], jnp.zeros((1, 256 - PAD), F32)], axis=1)
    rows = (g_bias[:1, :EDGE], g_bias[:1, EDGE:], second[:, :EDGE], second[:, EDGE:])
    last = jnp.zeros((16, EDGE), F32)
    for i, row in enumerate(rows):
        last = jnp.where(pick == i, row, last)
    end = 512 + 4 * PAD
    out[pl.ds(end, 16), :] = last.astype(BF16)
    out[pl.ds(end + 16, 1280 - 16 - end), :] = jnp.zeros((1280 - 16 - end, EDGE), BF16)


def add_pieces_kernel(x, out):
    total = x[0].astype(F32)
    for i in range(1, x.shape[0]):
        total = total + x[i].astype(F32)
    out[...] = total.astype(BF16)


def add_arrays_kernel(a, b, c, d, out):
    total = (a[...].astype(F32) + b[...].astype(F32)) + (c[...].astype(F32) + d[...].astype(F32))
    out[...] = total.astype(BF16)


def spread_kernel(a, b, c, d, out):
    total = (a[...].astype(F32) + b[...].astype(F32)) + (c[...].astype(F32) + d[...].astype(F32))
    for i in range(out.shape[0]):
        out[i] = total.astype(BF16)


def unpack_kernel(classes, x, self_first, neigh_first, bias_first, self_t, neigh_t, bias_second):
    self_first[...] = flip(x[pl.ds(0, 256), :])
    neigh_first[...] = flip(x[pl.ds(256, 256), :])
    for at, out in ((512, self_t), (512 + 2 * PAD, neigh_t)):
        for i in range(2):
            got = x[pl.ds(at + i * PAD, PAD), :].astype(F32)
            out[:, i * EDGE : (i + 1) * EDGE] = got[:classes]
    last = x[pl.ds(512 + 4 * PAD, 16), :].astype(F32)
    bias_first[...] = jnp.concatenate([last[0:1], last[1:2]], axis=1)
    bias_second[...] = jnp.concatenate([last[2:3], last[3:4]], axis=1)


def sum_everywhere(x):
    every = ("row", "col")
    number = lambda y, z, x, c: ((y * NZ + z) * 4 + x) * 2 + c
    groups = [
        [number(y, z, x, c) for y in range(NY) for x in range(4)] for z in range(NZ) for c in range(2)
    ]
    x = x.reshape(16, -1, EDGE)
    piece = jax.ShapeDtypeStruct(x.shape[1:], BF16)
    x = lax.all_to_all(x, every, 0, 0, tiled=True, axis_index_groups=groups)
    x = call(add_pieces_kernel, piece, [VMEM])(x)
    near = [lax.ppermute(x, every, [(i, i ^ flip_bits) for i in range(256)]) for flip_bits in (1, 8, 9)]
    x = call(add_arrays_kernel, piece, [VMEM] * 4)(x, *near)
    far = [lax.ppermute(x, "row", [(i, i ^ flip_bits) for i in range(32)]) for flip_bits in (2, 6, 4)]
    x = call(spread_kernel, jax.ShapeDtypeStruct((16, 80, EDGE), BF16), [VMEM] * 4)(x, *far)
    x = lax.all_to_all(x, every, 0, 0, tiled=True, axis_index_groups=groups)
    return x.reshape(-1, EDGE)


def on_device(
    features,
    tiles,
    block_rows,
    block_cols,
    labels,
    train_mask,
    self_first,
    neigh_first,
    bias_first,
    self_second,
    neigh_second,
    bias_second,
):
    classes = self_second.shape[1]
    hid_size = self_first.shape[1]
    scale = 1.0 / math.sqrt(65536)
    row, col = lax.axis_index("row"), lax.axis_index("col")
    tiles = tiles.reshape(-1, EDGE, EDGE)
    slots = slot_of(block_rows.reshape(-1), col)
    sources = block_cols.reshape(-1)
    cols = place_of(sources, row) * 2 + sources % 2
    offs = slots // 2 * 264 + slots % 2 * EDGE
    shape = jax.ShapeDtypeStruct
    dma = pltpu.SemaphoreType.DMA
    feat = features.reshape(2, EDGE, EDGE)
    n_groups = tiles.shape[0] // GROUP

    feat_parts = ring(jnp.concatenate(along_y(feat), axis=0), ALONG_Z)
    n_feat = len(feat_parts)
    degs = [
        call(
            functools.partial(degree_kernel, i * GROUP),
            shape((16, 8, EDGE), F32),
            [SMEM, VMEM],
            mib=4,
            flops=2**32,
            bytes_accessed=2**20,
        )(slots, tiles)
        for i in range(n_groups)
    ]
    block = shape((1056, EDGE), F32)
    keep, send = call(
        functools.partial(first_kernel, n_feat),
        (block, block),
        [SMEM] * 2 + [VMEM] * 5 + [ANY] * n_feat,
        [
            pltpu.VMEM((64, EDGE, EDGE), BF16),
            pltpu.VMEM((2112, EDGE), F32),
            dma((n_feat,)),
        ],
        mib=8,
        flops=2**29,
        bytes_accessed=2**23,
    )(offs, cols, tiles, *degs, *feat_parts)
    sums = call(join_first_kernel, (shape((264, EDGE), F32),) * 4, [VMEM] * 2)(
        keep, to_sibling(send)
    )
    agg, inv = call(
        aggregate_kernel, (shape((2, EDGE, EDGE), BF16), shape((2, EDGE), F32)), [VMEM] * 4
    )(sums[0], along_x(sums[1], 1), along_x(sums[2], 2), along_x(sums[3], 3))
    agg_parts = ring(jnp.concatenate(along_y(agg), axis=0), ALONG_Z)

    lacking = ((0, 256 - classes), (0, 0))
    self_t = jnp.pad(self_second.T, lacking)
    neigh_t = jnp.pad(neigh_second.T, lacking)
    square = shape((256, 256), BF16)
    weights, bias, self_wide, neigh_wide = call(
        weights_kernel,
        (square, shape((hid_size, EDGE), F32), square, square),
        [VMEM] * 4,
        flops=2**30,
    )(jnp.concatenate([self_first, neigh_first], axis=0), bias_first.reshape(1, -1), self_t, neigh_t)
    bias_wide = jnp.broadcast_to(jnp.pad(bias_second, (0, PAD - classes))[:, None], (PAD, EDGE))
    half = shape((8, PAD, EDGE), BF16)
    agg_second, keep, send, mine, hid = call(
        functools.partial(second_kernel, n_feat),
        (
            shape((16, hid_size, EDGE), BF16),
            half,
            half,
            shape((2, hid_size, EDGE), BF16),
            shape((64, hid_size, EDGE), BF16),
        ),
        [SMEM] * 2 + [VMEM] * (4 + 2 * n_feat),
        [pltpu.VMEM((16, hid_size, EDGE), F32)],
        mib=14,
        flops=2**31,
        bytes_accessed=2**23,
    )(slots, cols, tiles, neigh_t, weights, bias, *feat_parts, *agg_parts)
    sums = call(join_second_kernel, (shape((2, PAD, EDGE), BF16),) * 4, [VMEM] * 2)(
        keep, to_sibling(send)
    )
    lg, w, grad_self, grad_bias = call(
        functools.partial(loss_kernel, classes, scale),
        (
            shape((2, PAD, EDGE), BF16),
            shape((2, PAD, EDGE), BF16),
            shape((PAD, hid_size), F32),
            shape((8, PAD), F32),
        ),
        [VMEM] * 10,
    )(
        sums[0],
        along_x(sums[1], 1),
        along_x(sums[2], 2),
        along_x(sums[3], 3),
        mine,
        self_t,
        bias_wide,
        labels.reshape(2, EDGE),
        train_mask.reshape(2, EDGE),
        inv,
    )
    w_parts = [w, along_x(w, 1), along_x(w, 3), along_x(w, 2)]
    w_parts.append(to_sibling(jnp.concatenate(w_parts, axis=0)))
    grads = call(
        functools.partial(last_kernel, n_feat),
        shape((1280, EDGE), BF16),
        [SMEM] * 2 + [VMEM] * 13 + [ANY] * (2 * n_feat),
        [
            pltpu.VMEM((64, EDGE, 2 * EDGE), BF16),
            pltpu.VMEM((64, hid_size, EDGE), F32),
            pltpu.VMEM((16, hid_size, EDGE), BF16),
            dma((2 * n_feat,)),
        ],
        mib=22,
        flops=2**31,
        bytes_accessed=2**24,
    )(
        slots, cols, *w_parts, hid, tiles, agg_second, lg, self_wide, neigh_wide, grad_self,
        grad_bias, *feat_parts, *agg_parts
    )
    out = call(
        functools.partial(unpack_kernel, classes),
        (
            shape(self_first.shape, F32),
            shape(neigh_first.shape, F32),
            shape((1, hid_size), F32),
            shape((classes, hid_size), F32),
            shape((classes, hid_size), F32),
            shape((1, 256), F32),
        ),
        [VMEM],
    )(sum_everywhere(grads))
    return (
        out[0],
        out[1],
        out[2].reshape(hid_size),
        out[3].T,
        out[4].T,
        out[5].reshape(256)[:classes],
    )


def solution(mesh):
    in_specs = (
        P(("row", "col"), None),
        P("row", "col", None, None, None),
        P("row", "col", None),
        P("row", "col", None),
        P(("row", "col")),
        P(("row", "col")),
        P(),
        P(),
        P(),
        P(),
        P(),
        P(),
    )
    out_specs = (P(), P(), P(), P(), P(), P())
    return jax.shard_map(
        on_device, mesh=mesh, in_specs=in_specs, out_specs=out_specs, check_vma=False
    )
```
